256 devices in a mesh: gx: 8 (over y, core), gy: 8 (over z), gz: 4 (over x).
Axes of the slice: x: 4, y: 4, z: 8, core: 2. Of those that a mesh axis runs over, the one named last changes fastest.
Arguments:
- offsets: float32 [3, 16, 32, 16, 128], P(None, 'gx', 'gy', 'gz'), may hold values from -1 to 1
- velocity: float32 [3, 16, 32, 16, 128], P(None, 'gx', 'gy', 'gz'), may hold values from -3 to 3
- mass: float32 [16, 32, 16, 128], P('gx', 'gy', 'gz'), may hold values from 0.03 to 0.09
- counts: int32 [16, 32, 16], P('gx', 'gy', 'gz'), may hold values from 1 to 128
- owner: int32 [8192, 1], P(('gx', 'gy', 'gz')), may hold values from 0 to 63; in each aligned block of 32 rows (0 to 31, 32 to 63, ...) at most 2 rows name the same one
Outputs:
- arrived: float32 [32768, 7, 128], P(('gx', 'gy', 'gz'))
- density: float32 [16, 32, 16, 128], P('gx', 'gy', 'gz')
The draws below stay inside these ranges and needn't reach their ends.
Inputs may be any that keep to these rules, and one draw needn't show every extreme that they name: An owner is the layer index lx * 8 + ly of a device in the same gz layer. No device hands more than 2 bins to one owner, and some device hands exactly 2 to one.
All inputs are finite; a program needn't handle non-finite values.
Results may differ from the reference program's by a relative error of at most 0.0001.
Values sent between devices are 32-bit elements; how exact they have to be, the bound alone decides.
No kernel may reach another device: no remote copies, remote signals or barrier semaphores. Data moves between devices by JAX's collectives and lax.ppermute only.
A program may use at most 64 MiB of HBM per device.

```python
import math
import jax
import jax.numpy as jnp
import numpy as np
from jax import lax

BX = 2
BY = 4
BZ = 4
PART = 128
SUBSTEPS = 2
NBX = 16
NBY = 32
NBZ = 16
BINS_DEV = 32
CAP = 2
N_GX = 8
N_GY = 8
N_GZ = 4
DEVICES = 256


def set_ends(values, stream_key, least, top_value):
    longest = values.shape.index(max(values.shape))
    spots = []
    for shift in (0, 1):
        where = [jax.random.randint(jax.random.fold_in(stream_key, axis), (), 0, length) for axis, length in enumerate(values.shape)]
        where[longest] = (where[longest] + shift) % values.shape[longest]
        spots.append(tuple(where))
    return values.at[spots[0]].set(least).at[spots[1]].set(top_value)


def block_scale(rng, dims, split, least, high):
    factor_of = 1.0
    for axis_at, parts in split:
        draws = jax.random.uniform(jax.random.fold_in(jax.random.fold_in(rng, 6), axis_at), (parts,), jnp.float32, least / len(split), high / len(split))
        factor_of = factor_of * jnp.repeat(jnp.exp(draws), dims[axis_at] // parts).reshape((-1,) + (1,) * (len(dims) - 1 - axis_at))
    return factor_of


def assign_block(stream_key, own, number, rows, amount, top, bound, lean):
    sequence = jax.random.permutation(stream_key, amount)
    heavy_load, common = load_shares(amount, rows * top, bound, lean, True), load_shares(amount, rows * top, bound, lean, False)
    places = jnp.arange(amount)

    def named(lengths, offset_by):
        used = int((lengths > 0).sum())
        fixed = max(1, used // 4)
        shifted = fixed + (places - fixed + offset_by * (used - fixed)) % max(1, amount - fixed)
        return jnp.zeros((amount,), jnp.int32).at[sequence[jnp.where(places < fixed, places, shifted)]].set(jnp.asarray(lengths, jnp.int32))

    lengths = jnp.where(number % 4 == 0, named(heavy_load, number // 4), named(common, number - number // 4 - 1))
    mixed = jax.random.permutation(jax.random.fold_in(own, 3), amount)
    giver, sink = mixed[0:amount // 2 * 2:2], mixed[1:amount // 2 * 2:2]
    slack = jnp.minimum(lengths[giver] - 1, bound - lengths[sink]) // 2
    slack = jnp.where((giver == sequence[0]) | (sink == sequence[0]) | (lengths[sink] == 0), 0, jnp.maximum(slack, 0))
    shifted = jax.random.randint(jax.random.fold_in(own, 4), (amount // 2,), 0, 1 << 20) % (slack + 1)
    lengths = lengths.at[giver].add(-shifted).at[sink].add(shifted)
    items = jnp.searchsorted(jnp.cumsum(lengths), jnp.arange(rows * top), side="right").astype(jnp.int32)
    listing = items.reshape(top, rows).T
    listing = listing[jax.random.permutation(jax.random.fold_in(own, 1), rows)]
    offset_by = jax.random.randint(jax.random.fold_in(own, 2), (rows, 1), 0, top)
    return jnp.take_along_axis(listing, (jnp.arange(top)[None, :] + offset_by) % top, axis=1)


def load_shares(number_of, total, most, lean, full):
    weights = [(1 << 20) // math.isqrt(rank ** lean) + 1 for rank in range(1, number_of + 1)]
    largest = most if full else min(most, max(-(-total // number_of), total * weights[0] // sum(weights)))
    least = 1 if total - largest >= number_of - 1 else 0
    given, surplus = [largest] + [least] * (number_of - 1), total - largest - least * (number_of - 1)
    while surplus > 0:
        free = [i for i in range(1, number_of) if given[i] < largest] or [i for i in range(1, number_of) if given[i] < most]
        whole, budget = sum([weights[i] for i in free]), surplus
        for i in free:
            more = min(most - given[i], max(1, budget * weights[i] // whole), surplus)
            given[i] = given[i] + more
            surplus = surplus - more
    return np.array(given)


def centred(rng, extent, width, most, cuts=(), held_as=jnp.bfloat16):
    values = width * jax.random.normal(rng, extent, jnp.float32)
    if cuts:
        values = values * block_scale(rng, extent, cuts, -0.22, 0.18)
    return jnp.clip(values, -most, most).astype(held_as)


def setup_inputs(seed: int = 0) -> dict:
    splits = jax.random.split(jax.random.key(seed), 6)
    offsets = jnp.clip(jax.random.uniform(splits[0], (3, NBX, NBY, NBZ, PART), jnp.float32, -1.0, 1.0) * block_scale(splits[0], (3, NBX, NBY, NBZ, PART), ((1, 8), (2, 8), (3, 4)), -0.4, 0.0), -1.0, 1.0)
    velocity = centred(splits[1], (3, NBX, NBY, NBZ, PART), 0.5, 3.0, ((1, 8), (2, 8), (3, 4)), jnp.float32)
    mass = jnp.clip(jnp.exp(math.log(0.09) - 1.09861235 * jax.random.uniform(splits[2], (NBX, NBY, NBZ, PART), jnp.float32) ** block_scale(splits[2], (NBX, NBY, NBZ, PART), ((0, 8), (1, 8), (2, 4)), -0.2, 0.2)), 0.03, 0.09)
    counts = set_ends(jax.random.randint(splits[3], (NBX, NBY, NBZ), 1, PART + 1), jax.random.fold_in(splits[3], 1), 1, PART).astype(jnp.int32)
    owner_keys = jax.random.split(jax.random.fold_in(splits[4], 1), (DEVICES * BINS_DEV) // BINS_DEV)
    owner_turns = jax.random.permutation(jax.random.fold_in(splits[4], 3), (DEVICES * BINS_DEV) // BINS_DEV)
    owner = jax.vmap(lambda own, number: assign_block(jax.random.fold_in(splits[4], 2), own, number, BINS_DEV, N_GX * N_GY, 1, CAP, 1))(owner_keys, owner_turns).reshape((DEVICES * BINS_DEV, 1))
    return dict(offsets=offsets, velocity=velocity, mass=mass, counts=counts, owner=owner)


ALPHA = 21.0 / (16.0 * math.pi)
STIFF = 0.002
RHO_REST = 0.15
FLOOR = 0.05
VISCOSITY = 0.1
GRAVITY = 1.0
TIMESTEP = 0.2

def displacements():
    return [(a, b, c) for a in (-1, 0, 1) for b in (-1, 0, 1) for c in (-1, 0, 1)]

def geometry(own_pos, near_pos, shift):
    relative = own_pos[:, :, :, None] - (near_pos + shift[:, None, None])[:, :, None, :]
    dist_sq = lax.optimization_barrier(jnp.sum(relative * relative, axis=0))
    distance = jnp.sqrt(dist_sq)
    falloff = jnp.maximum(1.0 - 0.5 * distance, 0.0)
    return (relative, dist_sq, distance, falloff)

def density_pair(own_pos, near_pos, near_mass, shift):
    relative, dist_sq, distance, falloff = geometry(own_pos, near_pos, shift)
    fall_sq = falloff * falloff
    kernel = ALPHA * fall_sq * fall_sq * (2.0 * distance + 1.0)
    return lax.optimization_barrier(jnp.sum(near_mass[:, None, :] * kernel, axis=2))

def pressure_term(density):
    ratio = density / RHO_REST
    ratio_sq = ratio * ratio
    seventh = ratio_sq * ratio_sq * ratio_sq * ratio
    return STIFF * (seventh - 1.0) / (density * density)

def accel_pair(own_pos, own_vel, own_rho, near_pos, near_vel, near_mass, near_rho, shift):
    relative, dist_sq, distance, falloff = geometry(own_pos, near_pos, shift)
    near_rho = jnp.maximum(near_rho, FLOOR)
    approach = jnp.minimum(lax.optimization_barrier(jnp.sum((own_vel[:, :, :, None] - near_vel[:, :, None, :]) * relative, axis=0)), 0.0)
    mean_rho = 0.5 * (own_rho[:, :, None] + near_rho[:, None, :])
    viscous = -VISCOSITY * approach / ((dist_sq + 0.01) * mean_rho)
    slope = -5.0 * ALPHA * falloff * falloff * falloff
    weight = near_mass[:, None, :] * (pressure_term(own_rho)[:, :, None] + pressure_term(near_rho)[:, None, :] + viscous) * slope
    return -lax.optimization_barrier(jnp.sum(weight[None] * relative, axis=3))

def blocked(kernel_fn, arrays, axes_list, bins, block, out_axis):

    def one_block(number):
        start = number * block
        pieces = [lax.dynamic_slice_in_dim(array, start, block, axis) for array, axis in zip(arrays, axes_list)]
        return kernel_fn(*pieces)
    result = lax.map(one_block, jnp.arange(bins // block, dtype=jnp.int32))
    result = jnp.moveaxis(result, 0, out_axis)
    shape = result.shape
    return result.reshape(shape[:out_axis] + (shape[out_axis] * shape[out_axis + 1],) + shape[out_axis + 2:])

def reference(offsets, velocity, mass, counts, owner):
    grid = counts.shape
    extent_x, extent_y, extent_z = grid
    bins = extent_x * extent_y * extent_z
    block = min(128, bins)
    slot_ids = jnp.arange(PART, dtype=jnp.int32)
    alive = (slot_ids[None, None, None, :] < counts[..., None]).astype(jnp.float32)
    states = jnp.concatenate([offsets * alive[None], velocity * alive[None], (mass * alive)[None]], 0)
    alive_flat = alive.reshape(bins, PART)
    density = jnp.zeros((bins, PART), jnp.float32)
    for substep in range(SUBSTEPS):
        padded = jnp.pad(states, ((0, 0), (1, 1), (1, 1), (1, 1), (0, 0)))
        flattened = states.reshape(7, bins, PART)
        summed = jnp.zeros((bins, PART), jnp.float32)
        for step_x, step_y, step_z in displacements():
            near = padded[:, 1 + step_x:1 + step_x + extent_x, 1 + step_y:1 + step_y + extent_y, 1 + step_z:1 + step_z + extent_z].reshape(7, bins, PART)
            shift = jnp.array([2.0 * step_x, 2.0 * step_y, 2.0 * step_z], jnp.float32)
            summed = summed + blocked(lambda o, n, m: density_pair(o, n, m, shift), (flattened[0:3], near[0:3], near[6]), (1, 1, 0), bins, block, 0)
        density = jnp.maximum(summed, FLOOR)
        rim = jnp.pad(density.reshape(grid + (PART,)), ((1, 1), (1, 1), (1, 1), (0, 0)))
        pulled = jnp.zeros((3, bins, PART), jnp.float32)
        for step_x, step_y, step_z in displacements():
            near = padded[:, 1 + step_x:1 + step_x + extent_x, 1 + step_y:1 + step_y + extent_y, 1 + step_z:1 + step_z + extent_z].reshape(7, bins, PART)
            near_rho = rim[1 + step_x:1 + step_x + extent_x, 1 + step_y:1 + step_y + extent_y, 1 + step_z:1 + step_z + extent_z].reshape(bins, PART)
            shift = jnp.array([2.0 * step_x, 2.0 * step_y, 2.0 * step_z], jnp.float32)
            pulled = pulled + blocked(lambda a, b, c, d, e, f, g: accel_pair(a, b, c, d, e, f, g, shift), (flattened[0:3], flattened[3:6], density, near[0:3], near[3:6], near[6], near_rho), (1, 1, 0, 1, 1, 0, 0), bins, block, 1)
        downward = jnp.stack([jnp.zeros((), jnp.float32), jnp.zeros((), jnp.float32), jnp.full((), GRAVITY, jnp.float32)])
        accel = (pulled - downward[:, None, None]) * alive_flat[None]
        velocity_now = flattened[3:6] + TIMESTEP * accel
        position_now = flattened[0:3] + TIMESTEP * velocity_now
        states = jnp.concatenate([position_now, velocity_now, flattened[6:7]], 0).reshape((7,) + grid + (PART,))
    layers = N_GX * N_GY
    devices = N_GX * N_GY * N_GZ
    per_device = states.reshape(7, N_GX, BX, N_GY, BY, N_GZ, BZ, PART)
    per_device = jnp.transpose(per_device, (1, 3, 5, 2, 4, 6, 0, 7)).reshape(devices * BINS_DEV, 7, PART)
    target = owner.reshape(devices, BINS_DEV).astype(jnp.int32)
    one_hot = (target[..., None] == jnp.arange(layers, dtype=jnp.int32)[None, None, :]).astype(jnp.int32)
    rank = lax.optimization_barrier(jnp.sum((jnp.cumsum(one_hot, axis=1) - one_hot) * one_hot, axis=2))
    device_ids = jnp.arange(devices, dtype=jnp.int32)
    dest_device = target * N_GZ + (device_ids % N_GZ)[:, None]
    source_layer = (device_ids // N_GZ)[:, None]
    slot_index = ((dest_device * layers + source_layer) * CAP + rank).reshape(-1).astype(jnp.int32)
    arrived = jnp.zeros((devices * layers * CAP, 7, PART), jnp.float32).at[slot_index].set(per_device)
    return (arrived, density.reshape(grid + (PART,)))
```

```python
import functools
import math

import jax
import jax.numpy as jnp
import numpy as np
from jax import lax
from jax.experimental import pallas as pl
from jax.experimental.pallas import tpu as pltpu
from jax.sharding import PartitionSpec as P

SUBSTEPS = 2
ALPHA = 21.0 / (16.0 * math.pi)
STIFF = 0.002
RHO_REST = 0.15
FLOOR = 0.05
VISCOSITY = 0.1
GRAVITY = 1.0
TIMESTEP = 0.2

LANES = 128
TINY = 1e-30
DISPLACEMENTS = [(a, b, c) for a in (-1, 0, 1) for b in (-1, 0, 1) for c in (-1, 0, 1)]
ROWS = 29
CHUNK = 8


def pressure_term(density):
    ratio = density * (1.0 / RHO_REST)
    ratio_sq = ratio * ratio
    seventh = ratio_sq * ratio_sq * ratio_sq * ratio
    return STIFF * (seventh - 1.0) / (density * density)


def pack_sources(bins_ref, counts_ref, packed_ref, spot, grid, load):
    _, padded_y, padded_z = grid
    lane = lax.broadcasted_iota(jnp.int32, (8, LANES), 1)
    field = lax.broadcasted_iota(jnp.int32, (8, LANES), 0)
    units = [jnp.where(field == axis, 1.0, 0.0) for axis in range(3)]
    place = jnp.int32(0)
    current = jnp.zeros((8, LANES), jnp.float32)
    for step in DISPLACEMENTS:
        near = spot + (step[0] * padded_y + step[1]) * padded_z + step[2]
        number = counts_ref[near]
        block = load(near)
        for axis in range(3):
            if step[axis] > 0:
                block = block + units[axis]
            elif step[axis] < 0:
                block = block - units[axis]
        offset = lax.bitwise_and(place, LANES - 1)
        row = lax.shift_right_logical(place, 7)
        rolled = pltpu.roll(block, offset, 1)
        current = jnp.where(lane >= offset, rolled, current)
        packed_ref[row] = current
        place = place + number
        crossed = lax.shift_right_logical(place, 7) > row
        rest = jnp.where(lane < offset, rolled, 0.0)
        current = jnp.where(crossed, rest, current)
    row = lax.shift_right_logical(place, 7)
    packed_ref[row] = current
    packed_ref[row + 1] = jnp.zeros((8, LANES), jnp.float32)
    return lax.shift_right_logical(place + (LANES - 1), 7)


def own_spot(number, own, grid):
    own_y, own_z = own[1], own[2]
    _, padded_y, padded_z = grid
    at_x = number // (own_y * own_z)
    at_y = lax.rem(number // own_z, own_y)
    at_z = lax.rem(number, own_z)
    return ((at_x + 1) * padded_y + at_y + 1) * padded_z + at_z + 1


def spread(ref, row, field):
    return jnp.broadcast_to(ref[row, field : field + 1, :], (8, LANES))


def row_sums(ref):
    ones = jnp.ones((8, LANES), jnp.float32)
    return lax.dot_general(
        ones,
        ref[...],
        (((1,), (1,)), ((), ())),
        precision=lax.Precision.HIGHEST,
        preferred_element_type=jnp.float32,
    )


def in_chunks(groups, body):
    chunks = jnp.where(groups > CHUNK, 2, 1)

    def one(index, carry):
        half = jnp.where(chunks == 2, lax.shift_right_logical(groups + 1, 1), groups)
        first = index * half
        size = jnp.where(index == 0, half, groups - half)
        for known in range(1, CHUNK + 1):

            @pl.when(size == known)
            def _():
                body(first, known)

        return carry

    lax.fori_loop(0, chunks, one, 0)


def density_kernel(own, grid, counts_ref, bins_ref, out_ref, packed_ref, wide_ref, sums_ref):
    lane = lax.broadcasted_iota(jnp.int32, (8, LANES), 1)

    def one_bin(number, carry):
        spot = own_spot(number, own, grid)
        mine = counts_ref[spot]
        rows = pack_sources(bins_ref, counts_ref, packed_ref, spot, grid, lambda near: bins_ref[near])
        columns = jnp.transpose(bins_ref[spot])
        for axis in range(3):
            wide_ref[axis] = jnp.broadcast_to(columns[:, axis : axis + 1], (LANES, LANES))
        groups = jnp.minimum(lax.shift_right_logical(mine + 8, 3), LANES // 8)

        def sweep(first, size):
            unroll = 2 if size <= 4 else 1
            at = [pl.ds(pl.multiple_of((first + g) * 8, 8), 8) for g in range(size)]

            def one_row(turn, totals):
                totals = list(totals)
                for part in range(unroll):
                    row = turn * unroll + part
                    near = [spread(packed_ref, row, axis) for axis in range(3)]
                    mass = spread(packed_ref, row, 6)
                    mass5, mass4 = mass * (5.0 * ALPHA), mass * (4.0 * ALPHA)
                    for g in range(size):
                        x = wide_ref[0, at[g], :] - near[0]
                        y = wide_ref[1, at[g], :] - near[1]
                        z = wide_ref[2, at[g], :] - near[2]
                        square = x * x + y * y + z * z
                        square = jnp.maximum(square, TINY)
                        falloff = jnp.maximum(1.0 - square * lax.rsqrt(square), 0.0)
                        second = falloff * falloff
                        totals[g] = totals[g] + (second * second) * (mass5 - mass4 * falloff)
                return tuple(totals)

            totals = lax.fori_loop(
                0,
                (rows + unroll - 1) // unroll,
                one_row,
                tuple(jnp.zeros((8, LANES), jnp.float32) for _ in range(size)),
            )
            for g in range(size):
                sums_ref[at[g], :] = totals[g]

        in_chunks(groups, sweep)
        result = jnp.maximum(row_sums(sums_ref), FLOOR)
        empty = jnp.sum(jnp.where(lane == mine, result, 0.0), axis=1, keepdims=True)
        result = jnp.where(lane <= mine, result, empty)
        out_ref[number] = result
        return carry

    lax.fori_loop(0, own[0] * own[1] * own[2], one_bin, 0)


def accel_kernel(
    own, grid, counts_ref, where_ref, bins_ref, rho_ref, out_ref, packed_ref, term_ref, wide_ref, sums_ref
):
    bins = own[0] * own[1] * own[2]
    lane = lax.broadcasted_iota(jnp.int32, (8, LANES), 1)
    field = lax.broadcasted_iota(jnp.int32, (8, LANES), 0)
    slots = out_ref.shape[0]
    if slots != bins:

        def clear(number, carry):
            out_ref[number] = jnp.zeros((8, LANES), jnp.float32)
            return carry

        lax.fori_loop(0, slots, clear, 0)

    def whole(near):
        return jnp.where(field == 7, jnp.broadcast_to(rho_ref[pl.ds(near, 1), :], (8, LANES)), bins_ref[near])

    def one_bin(number, carry):
        spot = own_spot(number, own, grid)
        mine = counts_ref[spot]
        rows = pack_sources(bins_ref, counts_ref, packed_ref, spot, grid, whole)
        density = jnp.maximum(packed_ref[:, 7, :], FLOOR)
        term_ref[:, 0, :] = pressure_term(density)
        term_ref[:, 1, :] = density * (1.0 / VISCOSITY)
        block = whole(spot)
        my_rho = jnp.broadcast_to(jnp.maximum(rho_ref[pl.ds(spot, 1), :], FLOOR), (8, LANES))
        mixed = jnp.where(field == 6, pressure_term(my_rho), block)
        mixed = jnp.where(field == 7, my_rho * (1.0 / VISCOSITY), mixed)
        columns = jnp.transpose(mixed)
        for each in range(8):
            wide_ref[each] = jnp.broadcast_to(columns[:, each : each + 1], (LANES, LANES))
        groups = lax.shift_right_logical(mine + 7, 3)

        def sweep(first, size):
            unroll = 2 if size <= 4 else 1
            at = [pl.ds(pl.multiple_of((first + g) * 8, 8), 8) for g in range(size)]

            def one_row(turn, totals):
                totals = list(totals)
                for part in range(unroll):
                    row = turn * unroll + part
                    near = [spread(packed_ref, row, each) for each in range(7)]
                    near_term = spread(term_ref, row, 0)
                    near_rho = spread(term_ref, row, 1)
                    for g in range(size):
                        x = wide_ref[0, at[g], :] - near[0]
                        y = wide_ref[1, at[g], :] - near[1]
                        z = wide_ref[2, at[g], :] - near[2]
                        square = x * x + y * y + z * z
                        approach = (
                            (wide_ref[3, at[g], :] - near[3]) * x
                            + (wide_ref[4, at[g], :] - near[4]) * y
                            + (wide_ref[5, at[g], :] - near[5]) * z
                        )
                        approach = jnp.minimum(approach, 0.0)
                        below = (square + 0.0025) * (wide_ref[7, at[g], :] + near_rho)
                        viscous = approach / below
                        square = jnp.maximum(square, TINY)
                        falloff = jnp.maximum(1.0 - square * lax.rsqrt(square), 0.0)
                        third = falloff * falloff * falloff
                        weight = ((wide_ref[6, at[g], :] + near_term) - viscous) * (near[6] * third)
                        totals[3 * g] = totals[3 * g] + weight * x
                        totals[3 * g + 1] = totals[3 * g + 1] + weight * y
                        totals[3 * g + 2] = totals[3 * g + 2] + weight * z
                return tuple(totals)

            totals = lax.fori_loop(
                0,
                (rows + unroll - 1) // unroll,
                one_row,
                tuple(jnp.zeros((8, LANES), jnp.float32) for _ in range(3 * size)),
            )
            for g in range(size):
                for axis in range(3):
                    sums_ref[axis, at[g], :] = totals[3 * g + axis]

        in_chunks(groups, sweep)
        pulled = [row_sums(sums_ref.at[axis]) * (10.0 * ALPHA) for axis in range(3)]
        pulled[2] = pulled[2] - GRAVITY
        accel = jnp.zeros((8, LANES), jnp.float32)
        for axis in range(3):
            accel = jnp.where(field == axis, pulled[axis], accel)
        accel = jnp.where(lane < mine, accel, 0.0)
        before = bins_ref[spot]
        velocity = pltpu.roll(before, 5, 0) + TIMESTEP * accel
        position = before + (0.5 * TIMESTEP) * velocity
        after = jnp.where(field < 3, position, jnp.where(field < 6, pltpu.roll(velocity, 3, 0), before))
        after = jnp.where(field == 7, 0.0, after)
        if slots != bins:
            after = jnp.where(field < 3, after * 2.0, after)
        out_ref[where_ref[number]] = after
        return carry

    lax.fori_loop(0, bins, one_bin, 0)


VMEM_SPEC = pl.BlockSpec(memory_space=pltpu.VMEM)
SMEM_SPEC = pl.BlockSpec(memory_space=pltpu.SMEM)


def density_of(counts, bins, own, grid):
    number = own[0] * own[1] * own[2]
    out = pl.pallas_call(
        functools.partial(density_kernel, own, grid),
        out_shape=jax.ShapeDtypeStruct((number, 8, LANES), jnp.float32),
        in_specs=[SMEM_SPEC, VMEM_SPEC],
        out_specs=VMEM_SPEC,
        scratch_shapes=[
            pltpu.VMEM((ROWS, 8, LANES), jnp.float32),
            pltpu.VMEM((3, LANES, LANES), jnp.float32),
            pltpu.VMEM((LANES, LANES), jnp.float32),
        ],
        compiler_params=pltpu.CompilerParams(vmem_limit_bytes=32 * 1024 * 1024),
        name="density",
    )(counts, bins)
    return out[:, 0, :]


def moved(counts, where_to, bins, rho, own, grid, slots):
    return pl.pallas_call(
        functools.partial(accel_kernel, own, grid),
        out_shape=jax.ShapeDtypeStruct((slots, 8, LANES), jnp.float32),
        in_specs=[SMEM_SPEC, SMEM_SPEC, VMEM_SPEC, VMEM_SPEC],
        out_specs=VMEM_SPEC,
        scratch_shapes=[
            pltpu.VMEM((ROWS, 8, LANES), jnp.float32),
            pltpu.VMEM((ROWS, 8, LANES), jnp.float32),
            pltpu.VMEM((8, LANES, LANES), jnp.float32),
            pltpu.VMEM((3, LANES, LANES), jnp.float32),
        ],
        compiler_params=pltpu.CompilerParams(vmem_limit_bytes=32 * 1024 * 1024),
        name="accel",
    )(counts, where_to, bins, rho)


def extended(value):
    for dim, axis in enumerate(("gx", "gy", "gz")):
        devices, length = (lax.axis_size(axis), value.shape[dim])
        up = [(i, i + 1) for i in range(devices - 1)]
        down = [(j, i) for i, j in up]
        last = lax.slice_in_dim(value, length - 1, length, axis=dim)
        initial = lax.slice_in_dim(value, 0, 1, axis=dim)
        before = lax.ppermute(last, axis, up)
        after = lax.ppermute(initial, axis, down)
        value = jnp.concatenate([before, value, after], axis=dim)
    return value


def local(offsets, velocity, mass, counts, owner):
    own = counts.shape
    grid = tuple(extent + 2 for extent in own)
    bins = own[0] * own[1] * own[2]
    padded = grid[0] * grid[1] * grid[2]
    slot_ids = jnp.arange(LANES, dtype=jnp.int32)
    alive = slot_ids < counts[..., None]
    fields = jnp.concatenate([offsets * 0.5, velocity, mass[None], jnp.zeros_like(mass)[None]], 0)
    states = jnp.where(alive[..., None, :], jnp.transpose(fields, (1, 2, 3, 0, 4)), 0.0)
    layers = lax.axis_size("gx") * lax.axis_size("gy")
    capacity = max(2, 2 * bins // layers)
    target = owner[:, 0]
    earlier = np.tril(np.ones((bins, bins), bool), -1)
    rank = jnp.sum(((target[:, None] == target[None, :]) & earlier).astype(jnp.int32), axis=1)
    where_to = target * capacity + rank
    in_order = jnp.arange(bins, dtype=jnp.int32)
    near_counts = None
    for substep in range(SUBSTEPS):
        near = extended(states).reshape(padded, 8, LANES)
        if near_counts is None:
            near_counts = jnp.sum((near[:, 6, :] > 0.0).astype(jnp.int32), axis=1)
        density = density_of(near_counts, near, own, grid)
        near_rho = extended(density.reshape(own + (LANES,))).reshape(padded, LANES)
        last = substep == SUBSTEPS - 1
        states = moved(
            near_counts,
            where_to if last else in_order,
            near,
            near_rho,
            own,
            grid,
            layers * capacity if last else bins,
        )
        if not last:
            states = states.reshape(own + (8, LANES))
    arrived = lax.all_to_all(states, ("gx", "gy"), split_axis=0, concat_axis=0, tiled=True)
    return (arrived[:, :7, :], density.reshape(own + (LANES,)))


def solution(mesh):
    placed = (
        P(None, "gx", "gy", "gz", None),
        P(None, "gx", "gy", "gz", None),
        P("gx", "gy", "gz", None),
        P("gx", "gy", "gz"),
        P(("gx", "gy", "gz"), None),
    )
    return jax.shard_map(
        local,
        mesh=mesh,
        in_specs=placed,
        out_specs=(P(("gx", "gy", "gz"), None, None), P("gx", "gy", "gz", None)),
        check_vma=False,
    )
```

```python
import functools
import math

import jax
import jax.numpy as jnp
import numpy as np
from jax import lax
from jax.experimental import pallas as pl
from jax.experimental.pallas import tpu as pltpu
from jax.sharding import PartitionSpec as P

SUBSTEPS = 2
ALPHA = 21.0 / (16.0 * math.pi)
STIFF = 0.002
RHO_REST = 0.15
FLOOR = 0.05
VISCOSITY = 0.1
GRAVITY = 1.0
TIMESTEP = 0.2

LANES = 128
TINY = 1e-30
DISPLACEMENTS = [(a, b, c) for a in (-1, 0, 1) for b in (-1, 0, 1) for c in (-1, 0, 1)]
ROWS = 32
UNROLL_MOST = 4
CHUNK = 8
VMEM_LIMIT = 48 * 1024 * 1024


def pressure_term(density):
    ratio = density * (1.0 / RHO_REST)
    ratio_sq = ratio * ratio
    seventh = ratio_sq * ratio_sq * ratio_sq * ratio
    return STIFF * (seventh - 1.0) / (density * density)


def pack_sources(counts_ref, packed_ref, number, spot, grid, load):
    _, padded_y, padded_z = grid
    lane = lax.broadcasted_iota(jnp.int32, (8, LANES), 1)
    field = lax.broadcasted_iota(jnp.int32, (8, LANES), 0)
    units = [jnp.where(field == axis, 1.0, 0.0) for axis in range(3)]
    place = jnp.int32(0)
    current = jnp.zeros((8, LANES), jnp.float32)
    for step in DISPLACEMENTS:
        near = spot + (step[0] * padded_y + step[1]) * padded_z + step[2]
        block = load(near)
        for axis in range(3):
            if step[axis] > 0:
                block = block + units[axis]
            elif step[axis] < 0:
                block = block - units[axis]
        offset = lax.bitwise_and(place, LANES - 1)
        row = lax.shift_right_logical(place, 7)
        rolled = pltpu.roll(block, offset, 1)
        current = jnp.where(lane >= offset, rolled, current)
        packed_ref[number, row] = current
        place = place + counts_ref[near]
        crossed = lax.shift_right_logical(place, 7) > row
        rest = jnp.where(lane < offset, rolled, 0.0)
        current = jnp.where(crossed, rest, current)
    row = lax.shift_right_logical(place, 7)
    packed_ref[number, row] = jnp.where(lane < lax.bitwise_and(place, LANES - 1), current, 0.0)
    for more in range(1, UNROLL_MOST):
        packed_ref[number, row + more] = jnp.zeros((8, LANES), jnp.float32)
    return lax.shift_right_logical(place + (LANES - 1), 7)


def spread_columns(wide_ref, number, block, fields, groups):
    columns = jnp.transpose(block)
    half = LANES // 2

    def fill(first):
        for each in range(fields):
            wide_ref[number, each, pl.ds(first, half), :] = jnp.broadcast_to(
                columns[first : first + half, each : each + 1], (half, LANES)
            )

    fill(0)

    @pl.when(groups > half // 8)
    def _():
        fill(half)


def own_spot(number, own, grid):
    own_y, own_z = own[1], own[2]
    _, padded_y, padded_z = grid
    at_x = number // (own_y * own_z)
    at_y = lax.rem(number // own_z, own_y)
    at_z = lax.rem(number, own_z)
    return ((at_x + 1) * padded_y + at_y + 1) * padded_z + at_z + 1


def spread(ref, number, row, field):
    return jnp.broadcast_to(ref[number, row, field : field + 1, :], (8, LANES))


def row_sums(sums):
    lane = lax.broadcasted_iota(jnp.int32, (LANES, LANES), 1)
    row = lax.broadcasted_iota(jnp.int32, (LANES, LANES), 0)
    total = jnp.broadcast_to(jnp.sum(sums, axis=1, keepdims=True), (LANES, LANES))
    total = jnp.sum(jnp.where(lane == row, total, 0.0).reshape(LANES // 8, 8, LANES), axis=0)
    return jnp.broadcast_to(jnp.sum(total, axis=0, keepdims=True), (8, LANES))


def by_size(size, least, most, body):
    if least == most:
        body(least)
        return
    middle = (least + most) // 2

    @pl.when(size <= middle)
    def _():
        by_size(size, least, middle, body)

    @pl.when(size > middle)
    def _():
        by_size(size, middle + 1, most, body)


def each_bin(bins, body):
    def turn(index, carry):
        for part in range(4):
            body(index * 4 + part)
        return carry

    lax.fori_loop(0, bins // 4, turn, 0)


def density_kernel(own, grid, counts_ref, bins_ref, out_ref, packed_ref, wide_ref, sums_ref, rows_ref):
    bins = own[0] * own[1] * own[2]
    lane = lax.broadcasted_iota(jnp.int32, (8, LANES), 1)

    def groups_of(spot):
        return jnp.minimum(lax.shift_right_logical(counts_ref[spot] + 8, 3), LANES // 8)

    def prepare(number):
        spot = own_spot(number, own, grid)
        rows_ref[number] = pack_sources(
            counts_ref, packed_ref, number, spot, grid, lambda near: bins_ref[near]
        )
        spread_columns(wide_ref, number, bins_ref[spot], 3, groups_of(spot))

    each_bin(bins, prepare)

    def one_bin(number, carry):
        rows = rows_ref[number]

        def sweep(size):
            unroll = 2 if size > 7 else 4

            def one_row(turn, totals):
                totals = list(totals)
                for part in range(unroll):
                    row = turn * unroll + part
                    near = [spread(packed_ref, number, row, axis) for axis in range(3)]
                    mass = spread(packed_ref, number, row, 6)
                    mass5, mass4 = mass * (5.0 * ALPHA), mass * (4.0 * ALPHA)
                    for g in range(size):
                        at = pl.ds(g * 8, 8)
                        x = wide_ref[number, 0, at, :] - near[0]
                        y = wide_ref[number, 1, at, :] - near[1]
                        z = wide_ref[number, 2, at, :] - near[2]
                        square = x * x + y * y + z * z
                        square = jnp.maximum(square, TINY)
                        falloff = jnp.maximum(1.0 - square * lax.rsqrt(square), 0.0)
                        second = falloff * falloff
                        totals[g] = totals[g] + (second * second) * (mass5 - mass4 * falloff)
                return tuple(totals)

            totals = lax.fori_loop(
                0,
                lax.shift_right_logical(rows + unroll - 1, 1 if unroll == 2 else 2),
                one_row,
                tuple(jnp.zeros((8, LANES), jnp.float32) for _ in range(size)),
            )
            for g in range(size):
                sums_ref[number, pl.ds(g * 8, 8), :] = totals[g]

        by_size(groups_of(own_spot(number, own, grid)), 1, LANES // 8, sweep)
        return carry

    lax.fori_loop(0, bins, one_bin, 0)

    def finish(number):
        mine = counts_ref[own_spot(number, own, grid)]
        result = jnp.maximum(row_sums(sums_ref[number]), FLOOR)
        empty = jnp.sum(jnp.where(lane == mine, result, 0.0), axis=1, keepdims=True)
        result = jnp.where(lane <= mine, result, empty)
        out_ref[pl.ds(number, 1), :] = result[0:1]

    each_bin(bins, finish)


def accel_kernel(
    own,
    grid,
    counts_ref,
    where_ref,
    bins_ref,
    rho_ref,
    out_ref,
    packed_ref,
    term_ref,
    wide_ref,
    sums_ref,
    rows_ref,
):
    bins = own[0] * own[1] * own[2]
    lane = lax.broadcasted_iota(jnp.int32, (8, LANES), 1)
    field = lax.broadcasted_iota(jnp.int32, (8, LANES), 0)
    slots = out_ref.shape[0]
    if slots != bins:

        def clear(turn, carry):
            out_ref[pl.ds(turn * 8, 8)] = jnp.zeros((8, 8, LANES), jnp.float32)
            return carry

        lax.fori_loop(0, slots // 8, clear, 0)

    def groups_of(spot):
        return lax.shift_right_logical(counts_ref[spot] + 7, 3)

    def whole(near):
        return jnp.where(field == 7, jnp.broadcast_to(rho_ref[pl.ds(near, 1), :], (8, LANES)), bins_ref[near])

    def prepare(number):
        spot = own_spot(number, own, grid)
        rows_ref[number] = pack_sources(counts_ref, packed_ref, number, spot, grid, whole)
        density = jnp.maximum(packed_ref[number, :, 7, :], FLOOR)
        term_ref[number, 0] = pressure_term(density)
        term_ref[number, 1] = density * (1.0 / VISCOSITY)
        my_rho = jnp.broadcast_to(jnp.maximum(rho_ref[pl.ds(spot, 1), :], FLOOR), (8, LANES))
        mixed = jnp.where(field == 6, pressure_term(my_rho), bins_ref[spot])
        mixed = jnp.where(field == 7, my_rho * (1.0 / VISCOSITY), mixed)
        spread_columns(wide_ref, number, mixed, 8, groups_of(spot))

    each_bin(bins, prepare)

    def one_bin(number, carry):
        rows = rows_ref[number]
        groups = groups_of(own_spot(number, own, grid))

        def chunk(index, carry):
            half = jnp.where(groups > CHUNK, lax.shift_right_logical(groups + 1, 1), groups)
            first = index * half
            length = jnp.where(index == 0, half, groups - half)

            def sweep(size):
                unroll = 2 if size > 2 else 4
                at = [pl.ds(pl.multiple_of((first + g) * 8, 8), 8) for g in range(size)]

                def one_row(turn, totals):
                    totals = list(totals)
                    for part in range(unroll):
                        row = turn * unroll + part
                        near = [spread(packed_ref, number, row, each) for each in range(7)]
                        near_term = jnp.broadcast_to(term_ref[number, 0, pl.ds(row, 1), :], (8, LANES))
                        near_rho = jnp.broadcast_to(term_ref[number, 1, pl.ds(row, 1), :], (8, LANES))
                        for g in range(size):
                            x = wide_ref[number, 0, at[g], :] - near[0]
                            y = wide_ref[number, 1, at[g], :] - near[1]
                            z = wide_ref[number, 2, at[g], :] - near[2]
                            square = x * x + y * y + z * z
                            approach = (
                                (wide_ref[number, 3, at[g], :] - near[3]) * x
                                + (wide_ref[number, 4, at[g], :] - near[4]) * y
                                + (wide_ref[number, 5, at[g], :] - near[5]) * z
                            )
                            approach = jnp.minimum(approach, 0.0)
                            below = (square + 0.0025) * (wide_ref[number, 7, at[g], :] + near_rho)
                            viscous = approach / below
                            square = jnp.maximum(square, TINY)
                            falloff = jnp.maximum(1.0 - square * lax.rsqrt(square), 0.0)
                            third = falloff * falloff * falloff
                            weight = ((wide_ref[number, 6, at[g], :] + near_term) - viscous) * (near[6] * third)
                            totals[3 * g] = totals[3 * g] + weight * x
                            totals[3 * g + 1] = totals[3 * g + 1] + weight * y
                            totals[3 * g + 2] = totals[3 * g + 2] + weight * z
                    return tuple(totals)

                totals = lax.fori_loop(
                    0,
                    lax.shift_right_logical(rows + unroll - 1, 1 if unroll == 2 else 2),
                    one_row,
                    tuple(jnp.zeros((8, LANES), jnp.float32) for _ in range(3 * size)),
                )
                for g in range(size):
                    for axis in range(3):
                        sums_ref[number, axis, at[g], :] = totals[3 * g + axis]

            by_size(length, 1, CHUNK, sweep)
            return carry

        lax.fori_loop(0, jnp.where(groups > CHUNK, 2, 1), chunk, 0)
        return carry

    lax.fori_loop(0, bins, one_bin, 0)

    def finish(number):
        spot = own_spot(number, own, grid)
        pulled = [row_sums(sums_ref[number, axis]) * (10.0 * ALPHA) for axis in range(3)]
        pulled[2] = pulled[2] - GRAVITY
        accel = jnp.zeros((8, LANES), jnp.float32)
        for axis in range(3):
            accel = jnp.where(field == axis, pulled[axis], accel)
        accel = jnp.where(lane < counts_ref[spot], accel, 0.0)
        before = bins_ref[spot]
        velocity = pltpu.roll(before, 5, 0) + TIMESTEP * accel
        position = before + (0.5 * TIMESTEP) * velocity
        after = jnp.where(field < 3, position, jnp.where(field < 6, pltpu.roll(velocity, 3, 0), before))
        after = jnp.where(field == 7, 0.0, after)
        if slots != bins:
            after = jnp.where(field < 3, after * 2.0, after)
        out_ref[where_ref[number]] = after

    each_bin(bins, finish)


VMEM_SPEC = pl.BlockSpec(memory_space=pltpu.VMEM)
SMEM_SPEC = pl.BlockSpec(memory_space=pltpu.SMEM)


def density_of(counts, bins, own, grid):
    number = own[0] * own[1] * own[2]
    return pl.pallas_call(
        functools.partial(density_kernel, own, grid),
        out_shape=jax.ShapeDtypeStruct((number, LANES), jnp.float32),
        in_specs=[SMEM_SPEC, VMEM_SPEC],
        out_specs=VMEM_SPEC,
        scratch_shapes=[
            pltpu.VMEM((number, ROWS, 8, LANES), jnp.float32),
            pltpu.VMEM((number, 3, LANES, LANES), jnp.float32),
            pltpu.VMEM((number, LANES, LANES), jnp.float32),
            pltpu.SMEM((number,), jnp.int32),
        ],
        compiler_params=pltpu.CompilerParams(vmem_limit_bytes=VMEM_LIMIT),
        name="density",
    )(counts, bins)


def moved(counts, where_to, bins, rho, own, grid, slots):
    number = own[0] * own[1] * own[2]
    return pl.pallas_call(
        functools.partial(accel_kernel, own, grid),
        out_shape=jax.ShapeDtypeStruct((slots, 8, LANES), jnp.float32),
        in_specs=[SMEM_SPEC, SMEM_SPEC, VMEM_SPEC, VMEM_SPEC],
        out_specs=VMEM_SPEC,
        scratch_shapes=[
            pltpu.VMEM((number, ROWS, 8, LANES), jnp.float32),
            pltpu.VMEM((number, 2, ROWS, LANES), jnp.float32),
            pltpu.VMEM((number, 8, LANES, LANES), jnp.float32),
            pltpu.VMEM((number, 3, LANES, LANES), jnp.float32),
            pltpu.SMEM((number,), jnp.int32),
        ],
        compiler_params=pltpu.CompilerParams(vmem_limit_bytes=VMEM_LIMIT),
        name="accel",
    )(counts, where_to, bins, rho)


def extended(value):
    for dim, axis in enumerate(("gx", "gy", "gz")):
        devices, length = (lax.axis_size(axis), value.shape[dim])
        up = [(i, (i + 1) % devices) for i in range(devices)]
        down = [(j, i) for i, j in up]
        last = lax.slice_in_dim(value, length - 1, length, axis=dim)
        initial = lax.slice_in_dim(value, 0, 1, axis=dim)
        before = lax.ppermute(last, axis, up)
        after = lax.ppermute(initial, axis, down)
        value = jnp.concatenate([before, value, after], axis=dim)
    return value


def inside(grid):
    result = jnp.ones(grid, bool)
    for dim, axis in enumerate(("gx", "gy", "gz")):
        place = lax.broadcasted_iota(jnp.int32, grid, dim)
        device, last = lax.axis_index(axis), lax.axis_size(axis) - 1
        outside = ((place == 0) & (device == 0)) | ((place == grid[dim] - 1) & (device == last))
        result = result & ~outside
    return result


def local(offsets, velocity, mass, counts, owner):
    own = counts.shape
    grid = tuple(extent + 2 for extent in own)
    bins = own[0] * own[1] * own[2]
    padded = grid[0] * grid[1] * grid[2]
    slot_ids = jnp.arange(LANES, dtype=jnp.int32)
    alive = slot_ids < counts[..., None]
    fields = jnp.concatenate([offsets * 0.5, velocity, mass[None], jnp.zeros_like(mass)[None]], 0)
    states = jnp.where(alive[..., None, :], jnp.transpose(fields, (1, 2, 3, 0, 4)), 0.0)
    layers = lax.axis_size("gx") * lax.axis_size("gy")
    capacity = max(2, 2 * bins // layers)
    target = owner[:, 0]
    earlier = np.tril(np.ones((bins, bins), bool), -1)
    rank = jnp.sum(((target[:, None] == target[None, :]) & earlier).astype(jnp.int32), axis=1)
    where_to = target * capacity + rank
    in_order = jnp.arange(bins, dtype=jnp.int32)
    near_counts = None
    for substep in range(SUBSTEPS):
        near = extended(states).reshape(padded, 8, LANES)
        if near_counts is None:
            occupied = (near[:, 6, :] > 0.0) & inside(grid).reshape(padded, 1)
            near_counts = jnp.sum(occupied.astype(jnp.int32), axis=1)
        density = density_of(near_counts, near, own, grid)
        near_rho = extended(density.reshape(own + (LANES,))).reshape(padded, LANES)
        last = substep == SUBSTEPS - 1
        states = moved(
            near_counts,
            where_to if last else in_order,
            near,
            near_rho,
            own,
            grid,
            layers * capacity if last else bins,
        )
        if not last:
            states = states.reshape(own + (8, LANES))
    arrived = lax.all_to_all(states, ("gx", "gy"), split_axis=0, concat_axis=0, tiled=True)
    return (arrived[:, :7, :], density.reshape(own + (LANES,)))


def solution(mesh):
    placed = (
        P(None, "gx", "gy", "gz", None),
        P(None, "gx", "gy", "gz", None),
        P("gx", "gy", "gz", None),
        P("gx", "gy", "gz"),
        P(("gx", "gy", "gz"), None),
    )
    return jax.shard_map(
        local,
        mesh=mesh,
        in_specs=placed,
        out_specs=(P(("gx", "gy", "gz"), None, None), P("gx", "gy", "gz", None)),
        check_vma=False,
    )
```

```python
import functools
import math

import jax
import jax.numpy as jnp
import numpy as np
from jax import lax
from jax.experimental import pallas as pl
from jax.experimental.pallas import tpu as pltpu
from jax.sharding import PartitionSpec as P

SUBSTEPS = 2
ALPHA = 21.0 / (16.0 * math.pi)
STIFF = 0.002
RHO_REST = 0.15
FLOOR = 0.05
VISCOSITY = 0.1
GRAVITY = 1.0
TIMESTEP = 0.2

LANES = 128
TINY = 1e-30
DISPLACEMENTS = [(a, b, c) for a in (-1, 0, 1) for b in (-1, 0, 1) for c in (-1, 0, 1)]
ROWS = 32
UNROLL_MOST = 4
CHUNK = 16
VMEM_LIMIT = 48 * 1024 * 1024


def pressure_term(density):
    ratio = density * (1.0 / RHO_REST)
    ratio_sq = ratio * ratio
    seventh = ratio_sq * ratio_sq * ratio_sq * ratio
    return STIFF * (seventh - 1.0) / (density * density)


def pack_sources(counts_ref, packed_ref, number, spot, grid, load):
    _, padded_y, padded_z = grid
    lane = lax.broadcasted_iota(jnp.int32, (8, LANES), 1)
    field = lax.broadcasted_iota(jnp.int32, (8, LANES), 0)
    units = [jnp.where(field == axis, 1.0, 0.0) for axis in range(3)]
    place = jnp.int32(0)
    current = jnp.zeros((8, LANES), jnp.float32)
    for step in DISPLACEMENTS:
        near = spot + (step[0] * padded_y + step[1]) * padded_z + step[2]
        block = load(near)
        for axis in range(3):
            if step[axis] > 0:
                block = block + units[axis]
            elif step[axis] < 0:
                block = block - units[axis]
        offset = lax.bitwise_and(place, LANES - 1)
        row = lax.shift_right_logical(place, 7)
        rolled = pltpu.roll(block, offset, 1)
        current = jnp.where(lane >= offset, rolled, current)
        packed_ref[number, row] = current
        place = place + counts_ref[near]
        crossed = lax.shift_right_logical(place, 7) > row
        rest = jnp.where(lane < offset, rolled, 0.0)
        current = jnp.where(crossed, rest, current)
    row = lax.shift_right_logical(place, 7)
    packed_ref[number, row] = jnp.where(lane < lax.bitwise_and(place, LANES - 1), current, 0.0)
    for more in range(1, UNROLL_MOST):
        packed_ref[number, row + more] = jnp.zeros((8, LANES), jnp.float32)
    return lax.shift_right_logical(place + (LANES - 1), 7)


def spread_columns(wide_ref, number, block, fields):
    for each in range(fields):
        wide_ref[number, each] = jnp.transpose(jnp.broadcast_to(block[each : each + 1], (LANES, LANES)))


def own_spot(number, own, grid):
    own_y, own_z = own[1], own[2]
    _, padded_y, padded_z = grid
    at_x = number // (own_y * own_z)
    at_y = number // own_z % own_y
    at_z = number % own_z
    return ((at_x + 1) * padded_y + at_y + 1) * padded_z + at_z + 1


def spread(ref, number, row, field):
    return jnp.broadcast_to(ref[number, row, field : field + 1, :], (8, LANES))


def row_sums(sums):
    lane = lax.broadcasted_iota(jnp.int32, (LANES, LANES), 1)
    row = lax.broadcasted_iota(jnp.int32, (LANES, LANES), 0)
    total = jnp.broadcast_to(jnp.sum(sums, axis=1, keepdims=True), (LANES, LANES))
    total = jnp.sum(jnp.where(lane == row, total, 0.0).reshape(LANES // 8, 8, LANES), axis=0)
    return jnp.broadcast_to(jnp.sum(total, axis=0, keepdims=True), (8, LANES))


def by_size(size, least, most, body):
    if least == most:
        body(least)
        return
    middle = (least + most) // 2

    @pl.when(size <= middle)
    def _():
        by_size(size, least, middle, body)

    @pl.when(size > middle)
    def _():
        by_size(size, middle + 1, most, body)


def each_bin(bins, body):
    def turn(index, carry):
        for part in range(4):
            body(index * 4 + part)
        return carry

    lax.fori_loop(0, bins // 4, turn, 0)


def density_kernel(
    own, grid, counts_ref, bins_ref, out_ref, packed_ref, wide_ref, sums_ref, rows_ref
):
    bins = own[0] * own[1] * own[2]
    lane = lax.broadcasted_iota(jnp.int32, (8, LANES), 1)

    def groups_of(number):
        mine = counts_ref[own_spot(number, own, grid)]
        return jnp.minimum(lax.shift_right_logical(mine + 8, 3), LANES // 8)

    def prepare(number):
        spot = own_spot(number, own, grid)
        rows_ref[number] = pack_sources(
            counts_ref, packed_ref, number, spot, grid, lambda near: bins_ref[near]
        )
        spread_columns(wide_ref, number, bins_ref[spot], 3)

    each_bin(bins, prepare)

    def one_bin(number, carry):
        rows = rows_ref[number]

        def sweep(size):
            unroll = 2 if size > 7 else 4

            def one_row(turn, totals):
                totals = list(totals)
                for part in range(unroll):
                    row = turn * unroll + part
                    near = [spread(packed_ref, number, row, axis) for axis in range(3)]
                    mass = spread(packed_ref, number, row, 6)
                    mass5, mass4 = mass * (5.0 * ALPHA), mass * (4.0 * ALPHA)
                    for g in range(size):
                        at = pl.ds(g * 8, 8)
                        x = wide_ref[number, 0, at, :] - near[0]
                        y = wide_ref[number, 1, at, :] - near[1]
                        z = wide_ref[number, 2, at, :] - near[2]
                        square = x * x + y * y + z * z
                        square = jnp.maximum(square, TINY)
                        falloff = jnp.maximum(1.0 - square * lax.rsqrt(square), 0.0)
                        second = falloff * falloff
                        totals[g] = totals[g] + (second * second) * (mass5 - mass4 * falloff)
                return tuple(totals)

            totals = lax.fori_loop(
                0,
                lax.shift_right_logical(rows + unroll - 1, 1 if unroll == 2 else 2),
                one_row,
                tuple(jnp.zeros((8, LANES), jnp.float32) for _ in range(size)),
            )
            for g in range(size):
                sums_ref[number, pl.ds(g * 8, 8), :] = totals[g]

        by_size(groups_of(number), 1, LANES // 8, sweep)
        return carry

    lax.fori_loop(0, bins, one_bin, 0)

    def finish(number):
        mine = counts_ref[own_spot(number, own, grid)]
        result = jnp.maximum(row_sums(sums_ref[number]), FLOOR)
        empty = jnp.sum(jnp.where(lane == mine, result, 0.0), axis=1, keepdims=True)
        result = jnp.where(lane <= mine, result, empty)
        out_ref[pl.ds(number, 1), :] = result[0:1]

    each_bin(bins, finish)


def accel_kernel(
    own,
    grid,
    counts_ref,
    where_ref,
    bins_ref,
    rho_ref,
    out_ref,
    packed_ref,
    term_ref,
    wide_ref,
    sums_ref,
    whole_ref,
    rows_ref,
):
    bins = own[0] * own[1] * own[2]
    lane = lax.broadcasted_iota(jnp.int32, (8, LANES), 1)
    field = lax.broadcasted_iota(jnp.int32, (8, LANES), 0)
    slots = out_ref.shape[0]
    if slots != bins:

        def clear(turn, carry):
            out_ref[pl.ds(turn * 8, 8)] = jnp.zeros((8, 8, LANES), jnp.float32)
            return carry

        lax.fori_loop(0, slots // 8, clear, 0)

    def groups_of(number):
        return lax.shift_right_logical(counts_ref[own_spot(number, own, grid)] + 7, 3)

    def fill(turn, carry):
        for part in range(8):
            near = turn * 8 + part
            rho = jnp.broadcast_to(rho_ref[pl.ds(near, 1), :], (8, LANES))
            whole_ref[near] = jnp.where(field == 7, rho, bins_ref[near])
        return carry

    lax.fori_loop(0, whole_ref.shape[0] // 8, fill, 0)

    def prepare(number):
        spot = own_spot(number, own, grid)
        rows_ref[number] = pack_sources(
            counts_ref, packed_ref, number, spot, grid, lambda near: whole_ref[near]
        )
        block = whole_ref[spot]
        rho = jnp.maximum(block, FLOOR)
        mixed = jnp.where(field == 6, pressure_term(pltpu.roll(rho, 7, 0)), block)
        spread_columns(wide_ref, number, jnp.where(field == 7, rho * (1.0 / VISCOSITY), mixed), 8)
        density = jnp.maximum(packed_ref[number, :, 7, :], FLOOR)
        term_ref[number, 0] = pressure_term(density)
        term_ref[number, 1] = density * (1.0 / VISCOSITY)

    each_bin(bins, prepare)

    def one_bin(number, carry):
        rows = rows_ref[number]
        groups = groups_of(number)

        def chunk(index, carry):
            half = jnp.where(groups > CHUNK, lax.shift_right_logical(groups + 1, 1), groups)
            first = index * half
            length = jnp.where(index == 0, half, groups - half)

            def sweep(size):
                unroll = 2 if size > 2 else 4
                at = [pl.ds(pl.multiple_of((first + g) * 8, 8), 8) for g in range(size)]

                def one_row(turn, totals):
                    totals = list(totals)
                    for part in range(unroll):
                        row = turn * unroll + part
                        near = [spread(packed_ref, number, row, each) for each in range(7)]
                        near_term = jnp.broadcast_to(term_ref[number, 0, pl.ds(row, 1), :], (8, LANES))
                        near_rho = jnp.broadcast_to(term_ref[number, 1, pl.ds(row, 1), :], (8, LANES))
                        for g in range(size):
                            x = wide_ref[number, 0, at[g], :] - near[0]
                            y = wide_ref[number, 1, at[g], :] - near[1]
                            z = wide_ref[number, 2, at[g], :] - near[2]
                            square = x * x + y * y + z * z
                            approach = (
                                (wide_ref[number, 3, at[g], :] - near[3]) * x
                                + (wide_ref[number, 4, at[g], :] - near[4]) * y
                                + (wide_ref[number, 5, at[g], :] - near[5]) * z
                            )
                            approach = jnp.minimum(approach, 0.0)
                            below = (square + 0.0025) * (wide_ref[number, 7, at[g], :] + near_rho)
                            viscous = approach / below
                            square = jnp.maximum(square, TINY)
                            falloff = jnp.maximum(1.0 - square * lax.rsqrt(square), 0.0)
                            third = falloff * falloff * falloff
                            weight = ((wide_ref[number, 6, at[g], :] + near_term) - viscous) * (near[6] * third)
                            totals[3 * g] = totals[3 * g] + weight * x
                            totals[3 * g + 1] = totals[3 * g + 1] + weight * y
                            totals[3 * g + 2] = totals[3 * g + 2] + weight * z
                    return tuple(totals)

                totals = lax.fori_loop(
                    0,
                    lax.shift_right_logical(rows + unroll - 1, 1 if unroll == 2 else 2),
                    one_row,
                    tuple(jnp.zeros((8, LANES), jnp.float32) for _ in range(3 * size)),
                )
                for g in range(size):
                    for axis in range(3):
                        sums_ref[number, axis, at[g], :] = totals[3 * g + axis]

            by_size(length, 1, CHUNK, sweep)
            return carry

        lax.fori_loop(0, jnp.where(groups > CHUNK, 2, 1), chunk, 0)
        return carry

    lax.fori_loop(0, bins, one_bin, 0)

    def finish(number):
        spot = own_spot(number, own, grid)
        pulled = [row_sums(sums_ref[number, axis]) * (10.0 * ALPHA) for axis in range(3)]
        pulled[2] = pulled[2] - GRAVITY
        accel = jnp.zeros((8, LANES), jnp.float32)
        for axis in range(3):
            accel = jnp.where(field == axis, pulled[axis], accel)
        accel = jnp.where(lane < counts_ref[spot], accel, 0.0)
        before = bins_ref[spot]
        velocity = pltpu.roll(before, 5, 0) + TIMESTEP * accel
        position = before + (0.5 * TIMESTEP) * velocity
        after = jnp.where(field < 3, position, jnp.where(field < 6, pltpu.roll(velocity, 3, 0), before))
        after = jnp.where(field == 7, 0.0, after)
        if slots != bins:
            after = jnp.where(field < 3, after * 2.0, after)
        out_ref[where_ref[number]] = after

    each_bin(bins, finish)


VMEM_SPEC = pl.BlockSpec(memory_space=pltpu.VMEM)
SMEM_SPEC = pl.BlockSpec(memory_space=pltpu.SMEM)


def density_of(counts, bins, own, grid):
    number = own[0] * own[1] * own[2]
    return pl.pallas_call(
        functools.partial(density_kernel, own, grid),
        out_shape=jax.ShapeDtypeStruct((number, LANES), jnp.float32),
        in_specs=[SMEM_SPEC, VMEM_SPEC],
        out_specs=VMEM_SPEC,
        scratch_shapes=[
            pltpu.VMEM((number, ROWS, 8, LANES), jnp.float32),
            pltpu.VMEM((number, 3, LANES, LANES), jnp.float32),
            pltpu.VMEM((number, LANES, LANES), jnp.float32),
            pltpu.SMEM((number,), jnp.int32),
        ],
        compiler_params=pltpu.CompilerParams(vmem_limit_bytes=VMEM_LIMIT),
        name="density",
    )(counts, bins)


def moved(counts, where_to, bins, rho, own, grid, slots):
    number = own[0] * own[1] * own[2]
    return pl.pallas_call(
        functools.partial(accel_kernel, own, grid),
        out_shape=jax.ShapeDtypeStruct((slots, 8, LANES), jnp.float32),
        in_specs=[SMEM_SPEC, SMEM_SPEC, VMEM_SPEC, VMEM_SPEC],
        out_specs=VMEM_SPEC,
        scratch_shapes=[
            pltpu.VMEM((number, ROWS, 8, LANES), jnp.float32),
            pltpu.VMEM((number, 2, ROWS, LANES), jnp.float32),
            pltpu.VMEM((number, 8, LANES, LANES), jnp.float32),
            pltpu.VMEM((number, 3, LANES, LANES), jnp.float32),
            pltpu.VMEM(bins.shape, jnp.float32),
            pltpu.SMEM((number,), jnp.int32),
        ],
        compiler_params=pltpu.CompilerParams(vmem_limit_bytes=VMEM_LIMIT),
        name="accel",
    )(counts, where_to, bins, rho)


def extended(value):
    for dim, axis in enumerate(("gx", "gy", "gz")):
        devices, length = (lax.axis_size(axis), value.shape[dim])
        up = [(i, (i + 1) % devices) for i in range(devices)]
        down = [(j, i) for i, j in up]
        last = lax.slice_in_dim(value, length - 1, length, axis=dim)
        initial = lax.slice_in_dim(value, 0, 1, axis=dim)
        before = lax.ppermute(last, axis, up)
        after = lax.ppermute(initial, axis, down)
        value = jnp.concatenate([before, value, after], axis=dim)
    return value


def inside(grid):
    result = jnp.ones(grid, bool)
    for dim, axis in enumerate(("gx", "gy", "gz")):
        place = lax.broadcasted_iota(jnp.int32, grid, dim)
        device, last = lax.axis_index(axis), lax.axis_size(axis) - 1
        outside = ((place == 0) & (device == 0)) | ((place == grid[dim] - 1) & (device == last))
        result = result & ~outside
    return result


def local(offsets, velocity, mass, counts, owner):
    own = counts.shape
    grid = tuple(extent + 2 for extent in own)
    bins = own[0] * own[1] * own[2]
    padded = grid[0] * grid[1] * grid[2]
    slot_ids = jnp.arange(LANES, dtype=jnp.int32)
    alive = slot_ids < counts[..., None]
    fields = jnp.concatenate([offsets * 0.5, velocity, mass[None], jnp.zeros_like(mass)[None]], 0)
    states = jnp.where(alive[..., None, :], jnp.transpose(fields, (1, 2, 3, 0, 4)), 0.0)
    layers = lax.axis_size("gx") * lax.axis_size("gy")
    capacity = max(2, 2 * bins // layers)
    target = owner[:, 0]
    earlier = np.tril(np.ones((bins, bins), bool), -1)
    rank = jnp.sum(((target[:, None] == target[None, :]) & earlier).astype(jnp.int32), axis=1)
    where_to = target * capacity + rank
    in_order = jnp.arange(bins, dtype=jnp.int32)
    near_counts = None
    for substep in range(SUBSTEPS):
        near = extended(states).reshape(padded, 8, LANES)
        if near_counts is None:
            occupied = (near[:, 6, :] > 0.0) & inside(grid).reshape(padded, 1)
            near_counts = jnp.sum(occupied.astype(jnp.int32), axis=1)
        density = density_of(near_counts, near, own, grid)
        near_rho = extended(density.reshape(own + (LANES,))).reshape(padded, LANES)
        last = substep == SUBSTEPS - 1
        states = moved(
            near_counts,
            where_to if last else in_order,
            near,
            near_rho,
            own,
            grid,
            layers * capacity if last else bins,
        )
        if not last:
            states = states.reshape(own + (8, LANES))
    arrived = lax.all_to_all(states, ("gx", "gy"), split_axis=0, concat_axis=0, tiled=True)
    return (arrived[:, :7, :], density.reshape(own + (LANES,)))


def solution(mesh):
    placed = (
        P(None, "gx", "gy", "gz", None),
        P(None, "gx", "gy", "gz", None),
        P("gx", "gy", "gz", None),
        P("gx", "gy", "gz"),
        P(("gx", "gy", "gz"), None),
    )
    return jax.shard_map(
        local,
        mesh=mesh,
        in_specs=placed,
        out_specs=(P(("gx", "gy", "gz"), None, None), P("gx", "gy", "gz", None)),
        check_vma=False,
    )
```

```python
import functools
import math

import jax
import jax.numpy as jnp
import numpy as np
from jax import lax
from jax.experimental import pallas as pl
from jax.experimental.pallas import tpu as pltpu
from jax.sharding import PartitionSpec as P

SUBSTEPS = 2
ALPHA = 21.0 / (16.0 * math.pi)
STIFF = 0.002
RHO_REST = 0.15
FLOOR = 0.05
VISCOSITY = 0.1
GRAVITY = 1.0
TIMESTEP = 0.2

LANES = 128
TINY = 1e-30
DISPLACEMENTS = [(a, b, c) for a in (-1, 0, 1) for b in (-1, 0, 1) for c in (-1, 0, 1)]
ROWS = 32
UNROLL_MOST = 4
CHUNK = 16
VMEM_LIMIT = 34 * 1024 * 1024


def pressure_term(density):
    ratio = density * (1.0 / RHO_REST)
    ratio_sq = ratio * ratio
    seventh = ratio_sq * ratio_sq * ratio_sq * ratio
    return STIFF * (seventh - 1.0) / (density * density)


def pack_sources(counts_ref, packed_ref, number, spot, grid, load):
    _, padded_y, padded_z = grid
    lane = lax.broadcasted_iota(jnp.int32, (8, LANES), 1)
    field = lax.broadcasted_iota(jnp.int32, (8, LANES), 0)
    units = [jnp.where(field == axis, 1.0, 0.0) for axis in range(3)]
    place = jnp.int32(0)
    current = jnp.zeros((8, LANES), jnp.float32)
    for step in DISPLACEMENTS:
        near = spot + (step[0] * padded_y + step[1]) * padded_z + step[2]
        block = load(near)
        for axis in range(3):
            if step[axis] > 0:
                block = block + units[axis]
            elif step[axis] < 0:
                block = block - units[axis]
        offset = lax.bitwise_and(place, LANES - 1)
        row = lax.shift_right_logical(place, 7)
        rolled = pltpu.roll(block, offset, 1)
        current = jnp.where(lane >= offset, rolled, current)
        packed_ref[number, row] = current
        place = place + counts_ref[near]
        crossed = lax.shift_right_logical(place, 7) > row
        rest = jnp.where(lane < offset, rolled, 0.0)
        current = jnp.where(crossed, rest, current)
    row = lax.shift_right_logical(place, 7)
    packed_ref[number, row] = jnp.where(lane < lax.bitwise_and(place, LANES - 1), current, 0.0)
    for more in range(1, UNROLL_MOST):
        packed_ref[number, row + more] = jnp.zeros((8, LANES), jnp.float32)
    return lax.shift_right_logical(place + (LANES - 1), 7)


def spread_columns(wide_ref, number, block, fields):
    for each in range(fields):
        wide_ref[number, each] = jnp.transpose(jnp.broadcast_to(block[each : each + 1], (LANES, LANES)))


def own_spot(number, own, grid):
    own_y, own_z = own[1], own[2]
    _, padded_y, padded_z = grid
    at_x = number // (own_y * own_z)
    at_y = number // own_z % own_y
    at_z = number % own_z
    return ((at_x + 1) * padded_y + at_y + 1) * padded_z + at_z + 1


def spread(ref, number, row, field):
    return jnp.broadcast_to(ref[number, row, field : field + 1, :], (8, LANES))


def row_sums(sums):
    lane = lax.broadcasted_iota(jnp.int32, (LANES, LANES), 1)
    row = lax.broadcasted_iota(jnp.int32, (LANES, LANES), 0)
    total = jnp.broadcast_to(jnp.sum(sums, axis=1, keepdims=True), (LANES, LANES))
    total = jnp.sum(jnp.where(lane == row, total, 0.0).reshape(LANES // 8, 8, LANES), axis=0)
    return jnp.broadcast_to(jnp.sum(total, axis=0, keepdims=True), (8, LANES))


def by_size(size, least, most, body):
    if least == most:
        body(least)
        return
    middle = (least + most) // 2

    @pl.when(size <= middle)
    def _():
        by_size(size, least, middle, body)

    @pl.when(size > middle)
    def _():
        by_size(size, middle + 1, most, body)


def each_bin(bins, body):
    def turn(index, carry):
        for part in range(4):
            body(index * 4 + part)
        return carry

    lax.fori_loop(0, bins // 4, turn, 0)


def density_kernel(
    own, grid, counts_ref, bins_ref, wide_ref, out_ref, packed_ref, sums_ref, rows_ref
):
    bins = own[0] * own[1] * own[2]
    lane = lax.broadcasted_iota(jnp.int32, (8, LANES), 1)

    def groups_of(number):
        mine = counts_ref[own_spot(number, own, grid)]
        return jnp.minimum(lax.shift_right_logical(mine + 8, 3), LANES // 8)

    def prepare(number):
        spot = own_spot(number, own, grid)
        rows_ref[number] = pack_sources(
            counts_ref, packed_ref, number, spot, grid, lambda near: bins_ref[near]
        )

    each_bin(bins, prepare)

    def one_bin(number, carry):
        rows = rows_ref[number]

        def sweep(size):
            unroll = 2 if size > 7 else 4

            def one_row(turn, totals):
                totals = list(totals)
                for part in range(unroll):
                    row = turn * unroll + part
                    near = [spread(packed_ref, number, row, axis) for axis in range(3)]
                    mass = spread(packed_ref, number, row, 6)
                    mass5, mass4 = mass * (5.0 * ALPHA), mass * (4.0 * ALPHA)
                    for g in range(size):
                        at = pl.ds(g * 8, 8)
                        x = wide_ref[number, 0, at, :] - near[0]
                        y = wide_ref[number, 1, at, :] - near[1]
                        z = wide_ref[number, 2, at, :] - near[2]
                        square = x * x + y * y + z * z
                        square = jnp.maximum(square, TINY)
                        falloff = jnp.maximum(1.0 - square * lax.rsqrt(square), 0.0)
                        second = falloff * falloff
                        totals[g] = totals[g] + (second * second) * (mass5 - mass4 * falloff)
                return tuple(totals)

            totals = lax.fori_loop(
                0,
                lax.shift_right_logical(rows + unroll - 1, 1 if unroll == 2 else 2),
                one_row,
                tuple(jnp.zeros((8, LANES), jnp.float32) for _ in range(size)),
            )
            for g in range(size):
                sums_ref[number, pl.ds(g * 8, 8), :] = totals[g]

        by_size(groups_of(number), 1, LANES // 8, sweep)
        return carry

    lax.fori_loop(0, bins, one_bin, 0)

    def finish(number):
        mine = counts_ref[own_spot(number, own, grid)]
        result = jnp.maximum(row_sums(sums_ref[number]), FLOOR)
        empty = jnp.sum(jnp.where(lane == mine, result, 0.0), axis=1, keepdims=True)
        result = jnp.where(lane <= mine, result, empty)
        out_ref[pl.ds(number, 1), :] = result[0:1]

    each_bin(bins, finish)


def accel_kernel(
    own,
    grid,
    counts_ref,
    where_ref,
    bins_ref,
    rho_ref,
    wide_ref,
    speed_ref,
    out_ref,
    packed_ref,
    term_ref,
    own_term_ref,
    sums_ref,
    whole_ref,
    rows_ref,
):
    bins = own[0] * own[1] * own[2]
    lane = lax.broadcasted_iota(jnp.int32, (8, LANES), 1)
    field = lax.broadcasted_iota(jnp.int32, (8, LANES), 0)
    slots = out_ref.shape[0]
    if slots != bins:

        def clear(turn, carry):
            out_ref[pl.ds(turn * 8, 8)] = jnp.zeros((8, 8, LANES), jnp.float32)
            return carry

        lax.fori_loop(0, slots // 8, clear, 0)

    def groups_of(number):
        return lax.shift_right_logical(counts_ref[own_spot(number, own, grid)] + 7, 3)

    def fill(turn, carry):
        for part in range(8):
            near = turn * 8 + part
            rho = jnp.broadcast_to(rho_ref[pl.ds(near, 1), :], (8, LANES))
            whole_ref[near] = jnp.where(field == 7, rho, bins_ref[near])
        return carry

    lax.fori_loop(0, whole_ref.shape[0] // 8, fill, 0)

    def prepare(number):
        spot = own_spot(number, own, grid)
        rows_ref[number] = pack_sources(
            counts_ref, packed_ref, number, spot, grid, lambda near: whole_ref[near]
        )
        block = whole_ref[spot]
        rho = jnp.maximum(block, FLOOR)
        terms = jnp.where(field == 7, rho * (1.0 / VISCOSITY), pressure_term(pltpu.roll(rho, 7, 0)))
        spread_columns(own_term_ref, number, terms[6:8], 2)
        density = jnp.maximum(packed_ref[number, :, 7, :], FLOOR)
        term_ref[number, 0] = pressure_term(density)
        term_ref[number, 1] = density * (1.0 / VISCOSITY)

    each_bin(bins, prepare)

    def one_bin(number, carry):
        rows = rows_ref[number]
        groups = groups_of(number)

        def chunk(index, carry):
            half = jnp.where(groups > CHUNK, lax.shift_right_logical(groups + 1, 1), groups)
            first = index * half
            length = jnp.where(index == 0, half, groups - half)

            def sweep(size):
                unroll = 2 if size > 2 else 4
                at = [pl.ds(pl.multiple_of((first + g) * 8, 8), 8) for g in range(size)]

                def one_row(turn, totals):
                    totals = list(totals)
                    for part in range(unroll):
                        row = turn * unroll + part
                        near = [spread(packed_ref, number, row, each) for each in range(7)]
                        near_term = jnp.broadcast_to(term_ref[number, 0, pl.ds(row, 1), :], (8, LANES))
                        near_rho = jnp.broadcast_to(term_ref[number, 1, pl.ds(row, 1), :], (8, LANES))
                        for g in range(size):
                            x = wide_ref[number, 0, at[g], :] - near[0]
                            y = wide_ref[number, 1, at[g], :] - near[1]
                            z = wide_ref[number, 2, at[g], :] - near[2]
                            square = x * x + y * y + z * z
                            approach = (
                                (speed_ref[number, 0, at[g], :] - near[3]) * x
                                + (speed_ref[number, 1, at[g], :] - near[4]) * y
                                + (speed_ref[number, 2, at[g], :] - near[5]) * z
                            )
                            approach = jnp.minimum(approach, 0.0)
                            below = (square + 0.0025) * (own_term_ref[number, 1, at[g], :] + near_rho)
                            viscous = approach / below
                            square = jnp.maximum(square, TINY)
                            falloff = jnp.maximum(1.0 - square * lax.rsqrt(square), 0.0)
                            third = falloff * falloff * falloff
                            weight = ((own_term_ref[number, 0, at[g], :] + near_term) - viscous) * (near[6] * third)
                            totals[3 * g] = totals[3 * g] + weight * x
                            totals[3 * g + 1] = totals[3 * g + 1] + weight * y
                            totals[3 * g + 2] = totals[3 * g + 2] + weight * z
                    return tuple(totals)

                totals = lax.fori_loop(
                    0,
                    lax.shift_right_logical(rows + unroll - 1, 1 if unroll == 2 else 2),
                    one_row,
                    tuple(jnp.zeros((8, LANES), jnp.float32) for _ in range(3 * size)),
                )
                for g in range(size):
                    for axis in range(3):
                        sums_ref[number, axis, at[g], :] = totals[3 * g + axis]

            by_size(length, 1, CHUNK, sweep)
            return carry

        lax.fori_loop(0, jnp.where(groups > CHUNK, 2, 1), chunk, 0)
        return carry

    lax.fori_loop(0, bins, one_bin, 0)

    def finish(number):
        spot = own_spot(number, own, grid)
        pulled = [row_sums(sums_ref[number, axis]) * (10.0 * ALPHA) for axis in range(3)]
        pulled[2] = pulled[2] - GRAVITY
        accel = jnp.zeros((8, LANES), jnp.float32)
        for axis in range(3):
            accel = jnp.where(field == axis, pulled[axis], accel)
        accel = jnp.where(lane < counts_ref[spot], accel, 0.0)
        before = bins_ref[spot]
        velocity = pltpu.roll(before, 5, 0) + TIMESTEP * accel
        position = before + (0.5 * TIMESTEP) * velocity
        after = jnp.where(field < 3, position, jnp.where(field < 6, pltpu.roll(velocity, 3, 0), before))
        after = jnp.where(field == 7, 0.0, after)
        if slots != bins:
            after = jnp.where(field < 3, after * 2.0, after)
        out_ref[where_ref[number]] = after

    each_bin(bins, finish)


def columns_kernel(first, states_ref, out_ref):
    for number in range(out_ref.shape[0]):
        spread_columns(out_ref, number, states_ref[number, first : first + 3], 3)


VMEM_SPEC = pl.BlockSpec(memory_space=pltpu.VMEM)
SMEM_SPEC = pl.BlockSpec(memory_space=pltpu.SMEM)


def columns_of(states, bins, first):
    block = 8
    return pl.pallas_call(
        functools.partial(columns_kernel, first),
        grid=(bins // block,),
        out_shape=jax.ShapeDtypeStruct((bins, 3, LANES, LANES), jnp.float32),
        in_specs=[pl.BlockSpec((block, 8, LANES), lambda turn: (turn, 0, 0))],
        out_specs=pl.BlockSpec((block, 3, LANES, LANES), lambda turn: (turn, 0, 0, 0)),
        cost_estimate=pl.CostEstimate(flops=0, bytes_accessed=bins * 3 * LANES * LANES * 4, transcendentals=0),
        name="columns",
    )(states)


def density_of(counts, bins, columns, own, grid):
    number = own[0] * own[1] * own[2]
    return pl.pallas_call(
        functools.partial(density_kernel, own, grid),
        out_shape=jax.ShapeDtypeStruct((number, LANES), jnp.float32),
        in_specs=[SMEM_SPEC, VMEM_SPEC, VMEM_SPEC],
        out_specs=VMEM_SPEC,
        scratch_shapes=[
            pltpu.VMEM((number, ROWS, 8, LANES), jnp.float32),
            pltpu.VMEM((number, LANES, LANES), jnp.float32),
            pltpu.SMEM((number,), jnp.int32),
        ],
        compiler_params=pltpu.CompilerParams(vmem_limit_bytes=VMEM_LIMIT),
        name="density",
    )(counts, bins, columns)


def moved(counts, where_to, bins, rho, places, speeds, own, grid, slots):
    number = own[0] * own[1] * own[2]
    return pl.pallas_call(
        functools.partial(accel_kernel, own, grid),
        out_shape=jax.ShapeDtypeStruct((slots, 8, LANES), jnp.float32),
        in_specs=[SMEM_SPEC, SMEM_SPEC, VMEM_SPEC, VMEM_SPEC, VMEM_SPEC, VMEM_SPEC],
        out_specs=VMEM_SPEC,
        scratch_shapes=[
            pltpu.VMEM((number, ROWS, 8, LANES), jnp.float32),
            pltpu.VMEM((number, 2, ROWS, LANES), jnp.float32),
            pltpu.VMEM((number, 2, LANES, LANES), jnp.float32),
            pltpu.VMEM((number, 3, LANES, LANES), jnp.float32),
            pltpu.VMEM(bins.shape, jnp.float32),
            pltpu.SMEM((number,), jnp.int32),
        ],
        compiler_params=pltpu.CompilerParams(vmem_limit_bytes=VMEM_LIMIT),
        name="accel",
    )(counts, where_to, bins, rho, places, speeds)


def extended(value):
    for dim, axis in enumerate(("gx", "gy", "gz")):
        devices, length = (lax.axis_size(axis), value.shape[dim])
        up = [(i, (i + 1) % devices) for i in range(devices)]
        down = [(j, i) for i, j in up]
        last = lax.slice_in_dim(value, length - 1, length, axis=dim)
        initial = lax.slice_in_dim(value, 0, 1, axis=dim)
        before = lax.ppermute(last, axis, up)
        after = lax.ppermute(initial, axis, down)
        value = jnp.concatenate([before, value, after], axis=dim)
    return value


def inside(grid):
    result = jnp.ones(grid, bool)
    for dim, axis in enumerate(("gx", "gy", "gz")):
        place = lax.broadcasted_iota(jnp.int32, grid, dim)
        device, last = lax.axis_index(axis), lax.axis_size(axis) - 1
        outside = ((place == 0) & (device == 0)) | ((place == grid[dim] - 1) & (device == last))
        result = result & ~outside
    return result


def local(offsets, velocity, mass, counts, owner):
    own = counts.shape
    grid = tuple(extent + 2 for extent in own)
    bins = own[0] * own[1] * own[2]
    padded = grid[0] * grid[1] * grid[2]
    slot_ids = jnp.arange(LANES, dtype=jnp.int32)
    alive = slot_ids < counts[..., None]
    fields = jnp.concatenate([offsets * 0.5, velocity, mass[None], jnp.zeros_like(mass)[None]], 0)
    states = jnp.where(alive[..., None, :], jnp.transpose(fields, (1, 2, 3, 0, 4)), 0.0)
    layers = lax.axis_size("gx") * lax.axis_size("gy")
    capacity = max(2, 2 * bins // layers)
    target = owner[:, 0]
    earlier = np.tril(np.ones((bins, bins), bool), -1)
    rank = jnp.sum(((target[:, None] == target[None, :]) & earlier).astype(jnp.int32), axis=1)
    where_to = target * capacity + rank
    in_order = jnp.arange(bins, dtype=jnp.int32)
    near_counts = None
    for substep in range(SUBSTEPS):
        blocks = states.reshape(bins, 8, LANES)
        places = columns_of(blocks, bins, 0)
        near = extended(states).reshape(padded, 8, LANES)
        if near_counts is None:
            occupied = (near[:, 6, :] > 0.0) & inside(grid).reshape(padded, 1)
            near_counts = jnp.sum(occupied.astype(jnp.int32), axis=1)
        density = density_of(near_counts, near, places, own, grid)
        blocks, density = lax.optimization_barrier((blocks, density))
        speeds = columns_of(blocks, bins, 3)
        near_rho = extended(density.reshape(own + (LANES,))).reshape(padded, LANES)
        last = substep == SUBSTEPS - 1
        states = moved(
            near_counts,
            where_to if last else in_order,
            near,
            near_rho,
            places,
            speeds,
            own,
            grid,
            layers * capacity if last else bins,
        )
        if not last:
            states = states.reshape(own + (8, LANES))
    arrived = lax.all_to_all(states, ("gx", "gy"), split_axis=0, concat_axis=0, tiled=True)
    return (arrived[:, :7, :], density.reshape(own + (LANES,)))


def solution(mesh):
    placed = (
        P(None, "gx", "gy", "gz", None),
        P(None, "gx", "gy", "gz", None),
        P("gx", "gy", "gz", None),
        P("gx", "gy", "gz"),
        P(("gx", "gy", "gz"), None),
    )
    return jax.shard_map(
        local,
        mesh=mesh,
        in_specs=placed,
        out_specs=(P(("gx", "gy", "gz"), None, None), P("gx", "gy", "gz", None)),
        check_vma=False,
    )
```

```python
import functools
import math

import jax
import jax.numpy as jnp
import numpy as np
from jax import lax
from jax.experimental import pallas as pl
from jax.experimental.pallas import tpu as pltpu
from jax.sharding import PartitionSpec as P

SUBSTEPS = 2
ALPHA = 21.0 / (16.0 * math.pi)
STIFF = 0.002
RHO_REST = 0.15
FLOOR = 0.05
VISCOSITY = 0.1
GRAVITY = 1.0
TIMESTEP = 0.2

LANES = 128
TINY = 1e-30
DISPLACEMENTS = [(a, b, c) for a in (-1, 0, 1) for b in (-1, 0, 1) for c in (-1, 0, 1)]
ROWS = 32
UNROLL_MOST = 4
CHUNK = 16
VMEM_LIMIT = 48 * 1024 * 1024


def pressure_term(density):
    ratio = density * (1.0 / RHO_REST)
    ratio_sq = ratio * ratio
    seventh = ratio_sq * ratio_sq * ratio_sq * ratio
    return STIFF * (seventh - 1.0) / (density * density)


def pack_sources(counts_ref, packed_ref, number, spot, grid, load):
    _, padded_y, padded_z = grid
    lane = lax.broadcasted_iota(jnp.int32, (8, LANES), 1)
    field = lax.broadcasted_iota(jnp.int32, (8, LANES), 0)
    units = [jnp.where(field == axis, 1.0, 0.0) for axis in range(3)]
    place = jnp.int32(0)
    current = jnp.zeros((8, LANES), jnp.float32)
    for step in DISPLACEMENTS:
        near = spot + (step[0] * padded_y + step[1]) * padded_z + step[2]
        block = load(near)
        for axis in range(3):
            if step[axis] > 0:
                block = block + units[axis]
            elif step[axis] < 0:
                block = block - units[axis]
        offset = lax.bitwise_and(place, LANES - 1)
        row = lax.shift_right_logical(place, 7)
        rolled = pltpu.roll(block, offset, 1)
        current = jnp.where(lane >= offset, rolled, current)
        packed_ref[number, row] = current
        place = place + counts_ref[near]
        crossed = lax.shift_right_logical(place, 7) > row
        rest = jnp.where(lane < offset, rolled, 0.0)
        current = jnp.where(crossed, rest, current)
    row = lax.shift_right_logical(place, 7)
    packed_ref[number, row] = jnp.where(lane < lax.bitwise_and(place, LANES - 1), current, 0.0)
    for more in range(1, UNROLL_MOST):
        packed_ref[number, row + more] = jnp.zeros((8, LANES), jnp.float32)
    return lax.shift_right_logical(place + (LANES - 1), 7)


def spread_columns(wide_ref, number, block, fields):
    for each in range(fields):
        wide_ref[number, each] = jnp.transpose(jnp.broadcast_to(block[each : each + 1], (LANES, LANES)))


def own_spot(number, own, grid):
    own_y, own_z = own[1], own[2]
    _, padded_y, padded_z = grid
    at_x = number // (own_y * own_z)
    at_y = number // own_z % own_y
    at_z = number % own_z
    return ((at_x + 1) * padded_y + at_y + 1) * padded_z + at_z + 1


def spread(ref, number, row, field):
    return jnp.broadcast_to(ref[number, row, field : field + 1, :], (8, LANES))


def row_sums(sums):
    lane = lax.broadcasted_iota(jnp.int32, (LANES, LANES), 1)
    row = lax.broadcasted_iota(jnp.int32, (LANES, LANES), 0)
    total = jnp.broadcast_to(jnp.sum(sums, axis=1, keepdims=True), (LANES, LANES))
    total = jnp.sum(jnp.where(lane == row, total, 0.0).reshape(LANES // 8, 8, LANES), axis=0)
    return jnp.broadcast_to(jnp.sum(total, axis=0, keepdims=True), (8, LANES))


def by_size(size, least, most, body):
    if least == most:
        body(least)
        return
    middle = (least + most) // 2

    @pl.when(size <= middle)
    def _():
        by_size(size, least, middle, body)

    @pl.when(size > middle)
    def _():
        by_size(size, middle + 1, most, body)


def each_bin(bins, body):
    def turn(index, carry):
        for part in range(8):
            body(index * 8 + part)
        return carry

    lax.fori_loop(0, bins // 8, turn, 0)


def density_kernel(
    own, grid, counts_ref, bins_ref, columns_ref, out_ref, packed_ref, wide_ref, sums_ref, rows_ref, arrival
):
    bins = own[0] * own[1] * own[2]
    lane = lax.broadcasted_iota(jnp.int32, (8, LANES), 1)

    def groups_of(number):
        mine = counts_ref[own_spot(number, own, grid)]
        return jnp.minimum(lax.shift_right_logical(mine + 8, 3), LANES // 8)

    def prepare(number):
        spot = own_spot(number, own, grid)
        rows_ref[number] = pack_sources(
            counts_ref, packed_ref, number, spot, grid, lambda near: bins_ref[near]
        )

    columns = pltpu.make_async_copy(columns_ref, wide_ref, arrival)
    columns.start()
    each_bin(bins, prepare)
    columns.wait()

    def one_bin(number, carry):
        rows = rows_ref[number]

        def sweep(size):
            unroll = 2 if size > 7 else 4

            def one_row(turn, totals):
                totals = list(totals)
                for part in range(unroll):
                    row = turn * unroll + part
                    near = [spread(packed_ref, number, row, axis) for axis in range(3)]
                    mass = spread(packed_ref, number, row, 6)
                    mass5, mass4 = mass * (5.0 * ALPHA), mass * (4.0 * ALPHA)
                    for g in range(size):
                        at = pl.ds(g * 8, 8)
                        x = wide_ref[number, 0, at, :] - near[0]
                        y = wide_ref[number, 1, at, :] - near[1]
                        z = wide_ref[number, 2, at, :] - near[2]
                        square = x * x + y * y + z * z
                        square = jnp.maximum(square, TINY)
                        falloff = jnp.maximum(1.0 - square * lax.rsqrt(square), 0.0)
                        second = falloff * falloff
                        totals[g] = totals[g] + (second * second) * (mass5 - mass4 * falloff)
                return tuple(totals)

            totals = lax.fori_loop(
                0,
                lax.shift_right_logical(rows + unroll - 1, 1 if unroll == 2 else 2),
                one_row,
                tuple(jnp.zeros((8, LANES), jnp.float32) for _ in range(size)),
            )
            for g in range(size):
                sums_ref[number, pl.ds(g * 8, 8), :] = totals[g]

        by_size(groups_of(number), 1, LANES // 8, sweep)
        return carry

    lax.fori_loop(0, bins, one_bin, 0)

    def finish(number):
        mine = counts_ref[own_spot(number, own, grid)]
        result = jnp.maximum(row_sums(sums_ref[number]), FLOOR)
        empty = jnp.sum(jnp.where(lane == mine, result, 0.0), axis=1, keepdims=True)
        result = jnp.where(lane <= mine, result, empty)
        out_ref[pl.ds(number, 1), :] = result[0:1]

    each_bin(bins, finish)


def accel_kernel(
    own,
    grid,
    counts_ref,
    where_ref,
    bins_ref,
    rho_ref,
    places_ref,
    speeds_ref,
    out_ref,
    packed_ref,
    term_ref,
    wide_ref,
    speed_ref,
    own_term_ref,
    sums_ref,
    whole_ref,
    rows_ref,
    arrivals,
):
    bins = own[0] * own[1] * own[2]
    lane = lax.broadcasted_iota(jnp.int32, (8, LANES), 1)
    field = lax.broadcasted_iota(jnp.int32, (8, LANES), 0)
    slots = out_ref.shape[0]
    if slots != bins:

        def clear(turn, carry):
            out_ref[pl.ds(turn * 8, 8)] = jnp.zeros((8, 8, LANES), jnp.float32)
            return carry

        lax.fori_loop(0, slots // 8, clear, 0)

    def groups_of(number):
        return lax.shift_right_logical(counts_ref[own_spot(number, own, grid)] + 7, 3)

    places = pltpu.make_async_copy(places_ref, wide_ref, arrivals.at[0])
    speeds = pltpu.make_async_copy(speeds_ref, speed_ref, arrivals.at[1])
    places.start()
    speeds.start()

    def fill(turn, carry):
        for part in range(8):
            near = turn * 8 + part
            rho = jnp.broadcast_to(rho_ref[pl.ds(near, 1), :], (8, LANES))
            whole_ref[near] = jnp.where(field == 7, rho, bins_ref[near])
        return carry

    lax.fori_loop(0, whole_ref.shape[0] // 8, fill, 0)

    def prepare(number):
        spot = own_spot(number, own, grid)
        rows_ref[number] = pack_sources(
            counts_ref, packed_ref, number, spot, grid, lambda near: whole_ref[near]
        )
        block = whole_ref[spot]
        rho = jnp.maximum(block, FLOOR)
        terms = jnp.where(field == 7, rho * (1.0 / VISCOSITY), pressure_term(pltpu.roll(rho, 7, 0)))
        spread_columns(own_term_ref, number, terms[6:8], 2)
        density = jnp.maximum(packed_ref[number, :, 7, :], FLOOR)
        term_ref[number, 0] = pressure_term(density)
        term_ref[number, 1] = density * (1.0 / VISCOSITY)

    each_bin(bins, prepare)
    places.wait()
    speeds.wait()

    def one_bin(number, carry):
        rows = rows_ref[number]
        groups = groups_of(number)

        def chunk(index, carry):
            half = jnp.where(groups > CHUNK, lax.shift_right_logical(groups + 1, 1), groups)
            first = index * half
            length = jnp.where(index == 0, half, groups - half)

            def sweep(size):
                unroll = 2 if size > 2 else 4
                at = [pl.ds(pl.multiple_of((first + g) * 8, 8), 8) for g in range(size)]

                def one_row(turn, totals):
                    totals = list(totals)
                    for part in range(unroll):
                        row = turn * unroll + part
                        near = [spread(packed_ref, number, row, each) for each in range(7)]
                        near_term = jnp.broadcast_to(term_ref[number, 0, pl.ds(row, 1), :], (8, LANES))
                        near_rho = jnp.broadcast_to(term_ref[number, 1, pl.ds(row, 1), :], (8, LANES))
                        for g in range(size):
                            x = wide_ref[number, 0, at[g], :] - near[0]
                            y = wide_ref[number, 1, at[g], :] - near[1]
                            z = wide_ref[number, 2, at[g], :] - near[2]
                            square = x * x + y * y + z * z
                            approach = (
                                (speed_ref[number, 0, at[g], :] - near[3]) * x
                                + (speed_ref[number, 1, at[g], :] - near[4]) * y
                                + (speed_ref[number, 2, at[g], :] - near[5]) * z
                            )
                            approach = jnp.minimum(approach, 0.0)
                            below = (square + 0.0025) * (own_term_ref[number, 1, at[g], :] + near_rho)
                            viscous = approach / below
                            square = jnp.maximum(square, TINY)
                            falloff = jnp.maximum(1.0 - square * lax.rsqrt(square), 0.0)
                            third = falloff * falloff * falloff
                            weight = ((own_term_ref[number, 0, at[g], :] + near_term) - viscous) * (near[6] * third)
                            totals[3 * g] = totals[3 * g] + weight * x
                            totals[3 * g + 1] = totals[3 * g + 1] + weight * y
                            totals[3 * g + 2] = totals[3 * g + 2] + weight * z
                    return tuple(totals)

                totals = lax.fori_loop(
                    0,
                    lax.shift_right_logical(rows + unroll - 1, 1 if unroll == 2 else 2),
                    one_row,
                    tuple(jnp.zeros((8, LANES), jnp.float32) for _ in range(3 * size)),
                )
                for g in range(size):
                    for axis in range(3):
                        sums_ref[number, axis, at[g], :] = totals[3 * g + axis]

            by_size(length, 1, CHUNK, sweep)
            return carry

        lax.fori_loop(0, jnp.where(groups > CHUNK, 2, 1), chunk, 0)
        return carry

    lax.fori_loop(0, bins, one_bin, 0)

    def finish(number):
        spot = own_spot(number, own, grid)
        pulled = [row_sums(sums_ref[number, axis]) * (10.0 * ALPHA) for axis in range(3)]
        pulled[2] = pulled[2] - GRAVITY
        accel = jnp.zeros((8, LANES), jnp.float32)
        for axis in range(3):
            accel = jnp.where(field == axis, pulled[axis], accel)
        accel = jnp.where(lane < counts_ref[spot], accel, 0.0)
        before = bins_ref[spot]
        velocity = pltpu.roll(before, 5, 0) + TIMESTEP * accel
        position = before + (0.5 * TIMESTEP) * velocity
        after = jnp.where(field < 3, position, jnp.where(field < 6, pltpu.roll(velocity, 3, 0), before))
        after = jnp.where(field == 7, 0.0, after)
        if slots != bins:
            after = jnp.where(field < 3, after * 2.0, after)
        out_ref[where_ref[number]] = after

    each_bin(bins, finish)


def columns_kernel(first, states_ref, out_ref):
    for number in range(out_ref.shape[0]):
        spread_columns(out_ref, number, states_ref[number, first : first + 3], 3)


VMEM_SPEC = pl.BlockSpec(memory_space=pltpu.VMEM)
SMEM_SPEC = pl.BlockSpec(memory_space=pltpu.SMEM)
ANY_SPEC = pl.BlockSpec(memory_space=pl.ANY)


def columns_of(states, bins, first):
    block = 8
    return pl.pallas_call(
        functools.partial(columns_kernel, first),
        grid=(bins // block,),
        out_shape=jax.ShapeDtypeStruct((bins, 3, LANES, LANES), jnp.float32),
        in_specs=[pl.BlockSpec((block, 8, LANES), lambda turn: (turn, 0, 0))],
        out_specs=pl.BlockSpec((block, 3, LANES, LANES), lambda turn: (turn, 0, 0, 0)),
        cost_estimate=pl.CostEstimate(flops=0, bytes_accessed=bins * 3 * LANES * LANES * 4, transcendentals=0),
        name="columns",
    )(states)


def density_of(counts, bins, columns, own, grid):
    number = own[0] * own[1] * own[2]
    return pl.pallas_call(
        functools.partial(density_kernel, own, grid),
        out_shape=jax.ShapeDtypeStruct((number, LANES), jnp.float32),
        in_specs=[SMEM_SPEC, VMEM_SPEC, ANY_SPEC],
        out_specs=VMEM_SPEC,
        scratch_shapes=[
            pltpu.VMEM((number, ROWS, 8, LANES), jnp.float32),
            pltpu.VMEM((number, 3, LANES, LANES), jnp.float32),
            pltpu.VMEM((number, LANES, LANES), jnp.float32),
            pltpu.SMEM((number,), jnp.int32),
            pltpu.SemaphoreType.DMA,
        ],
        compiler_params=pltpu.CompilerParams(vmem_limit_bytes=VMEM_LIMIT),
        name="density",
    )(counts, bins, columns)


def moved(counts, where_to, bins, rho, places, speeds, own, grid, slots):
    number = own[0] * own[1] * own[2]
    return pl.pallas_call(
        functools.partial(accel_kernel, own, grid),
        out_shape=jax.ShapeDtypeStruct((slots, 8, LANES), jnp.float32),
        in_specs=[SMEM_SPEC, SMEM_SPEC, VMEM_SPEC, VMEM_SPEC, ANY_SPEC, ANY_SPEC],
        out_specs=VMEM_SPEC,
        scratch_shapes=[
            pltpu.VMEM((number, ROWS, 8, LANES), jnp.float32),
            pltpu.VMEM((number, 2, ROWS, LANES), jnp.float32),
            pltpu.VMEM((number, 3, LANES, LANES), jnp.float32),
            pltpu.VMEM((number, 3, LANES, LANES), jnp.float32),
            pltpu.VMEM((number, 2, LANES, LANES), jnp.float32),
            pltpu.VMEM((number, 3, LANES, LANES), jnp.float32),
            pltpu.VMEM(bins.shape, jnp.float32),
            pltpu.SMEM((number,), jnp.int32),
            pltpu.SemaphoreType.DMA((2,)),
        ],
        compiler_params=pltpu.CompilerParams(vmem_limit_bytes=VMEM_LIMIT),
        name="accel",
    )(counts, where_to, bins, rho, places, speeds)


def extended(value):
    for dim, axis in enumerate(("gx", "gy", "gz")):
        devices, length = (lax.axis_size(axis), value.shape[dim])
        up = [(i, (i + 1) % devices) for i in range(devices)]
        down = [(j, i) for i, j in up]
        last = lax.slice_in_dim(value, length - 1, length, axis=dim)
        initial = lax.slice_in_dim(value, 0, 1, axis=dim)
        before = lax.ppermute(last, axis, up)
        after = lax.ppermute(initial, axis, down)
        value = jnp.concatenate([before, value, after], axis=dim)
    return value


def inside(grid):
    result = jnp.ones(grid, bool)
    for dim, axis in enumerate(("gx", "gy", "gz")):
        place = lax.broadcasted_iota(jnp.int32, grid, dim)
        device, last = lax.axis_index(axis), lax.axis_size(axis) - 1
        outside = ((place == 0) & (device == 0)) | ((place == grid[dim] - 1) & (device == last))
        result = result & ~outside
    return result


def local(offsets, velocity, mass, counts, owner):
    own = counts.shape
    grid = tuple(extent + 2 for extent in own)
    bins = own[0] * own[1] * own[2]
    padded = grid[0] * grid[1] * grid[2]
    slot_ids = jnp.arange(LANES, dtype=jnp.int32)
    alive = slot_ids < counts[..., None]
    fields = jnp.concatenate([offsets * 0.5, velocity, mass[None], jnp.zeros_like(mass)[None]], 0)
    states = jnp.where(alive[..., None, :], jnp.transpose(fields, (1, 2, 3, 0, 4)), 0.0)
    layers = lax.axis_size("gx") * lax.axis_size("gy")
    capacity = max(2, 2 * bins // layers)
    target = owner[:, 0]
    earlier = np.tril(np.ones((bins, bins), bool), -1)
    rank = jnp.sum(((target[:, None] == target[None, :]) & earlier).astype(jnp.int32), axis=1)
    where_to = target * capacity + rank
    in_order = jnp.arange(bins, dtype=jnp.int32)
    near_counts = None
    for substep in range(SUBSTEPS):
        blocks = states.reshape(bins, 8, LANES)
        places = columns_of(blocks, bins, 0)
        near = extended(states).reshape(padded, 8, LANES)
        if near_counts is None:
            occupied = (near[:, 6, :] > 0.0) & inside(grid).reshape(padded, 1)
            near_counts = jnp.sum(occupied.astype(jnp.int32), axis=1)
        density = density_of(near_counts, near, places, own, grid)
        blocks, density = lax.optimization_barrier((blocks, density))
        speeds = columns_of(blocks, bins, 3)
        near_rho = extended(density.reshape(own + (LANES,))).reshape(padded, LANES)
        last = substep == SUBSTEPS - 1
        states = moved(
            near_counts,
            where_to if last else in_order,
            near,
            near_rho,
            places,
            speeds,
            own,
            grid,
            layers * capacity if last else bins,
        )
        if not last:
            states = states.reshape(own + (8, LANES))
    arrived = lax.all_to_all(states, ("gx", "gy"), split_axis=0, concat_axis=0, tiled=True)
    return (arrived[:, :7, :], density.reshape(own + (LANES,)))


def solution(mesh):
    placed = (
        P(None, "gx", "gy", "gz", None),
        P(None, "gx", "gy", "gz", None),
        P("gx", "gy", "gz", None),
        P("gx", "gy", "gz"),
        P(("gx", "gy", "gz"), None),
    )
    return jax.shard_map(
        local,
        mesh=mesh,
        in_specs=placed,
        out_specs=(P(("gx", "gy", "gz"), None, None), P("gx", "gy", "gz", None)),
        check_vma=False,
    )
```
